32 devices in a mesh: group: 4 (over z), req: 8 (over y, x, core).
Axes of the slice: x: 2, y: 2, z: 4, core: 2. Of those that a mesh axis runs over, the one named last changes fastest.
Arguments:
- layer_input: bfloat16 [4096, 3072], P(('group', 'req')), may hold values from -6 to 6
- queries: bfloat16 [4096, 3072], P(('group', 'req')), may hold values from -240 to 240, as said below
- suffix_kv: bfloat16 [4096, 2048], P(('group', 'req')), may hold values from -6 to 6
- past_kv: bfloat16 [8192, 2048], P(('group', 'req')), may hold values from -6 to 6
- prefix_kv: bfloat16 [512, 2048], P(('group', 'req')), may hold values from -6 to 6
- suffix_len: int32 [32], P(('group', 'req')), may hold values from 1 to 128, 3072 in all
- past_len: int32 [32], P(('group', 'req')), may hold values from 1 to 256, 4096 in all
- out_weight: bfloat16 [3072, 3072], P('group'), may hold values from -0.109375 to 0.109375
- norm_gain: bfloat16 [3072], replicated, may hold values from 0.5 to 1.5
- gate_weight: bfloat16 [3072, 8192], P(None, 'req'), may hold values from -0.109375 to 0.109375
- up_weight: bfloat16 [3072, 8192], P(None, 'req'), may hold values from -0.109375 to 0.109375
- down_weight: bfloat16 [8192, 3072], P('req'), may hold values from -0.0625 to 0.0625
Outputs:
- layer_output: bfloat16 [4096, 3072], P(('group', 'req'))
The draws below stay inside these ranges and needn't reach their ends.
Inputs may be any that keep to these rules, and one draw needn't show every extreme that they name: `queries`: normally distributed entries; some rows may be far larger.
All inputs are finite; a program needn't handle non-finite values. No bound on the sum of `suffix_len` or of `past_len` on one device may be relied on, other than what follows from the above.
Results may differ from the reference program's by a relative error of at most 0.012.
Values may be sent and summed in bfloat16 or wider, within the bound.
A program may use at most 128 MiB of HBM per device.

```python
import math
import jax
import jax.numpy as jnp
import numpy as np
from jax import lax

D = 3072
HEADS = 24
KV_HEADS = 8
HEAD = 128
FF = 8192
TOK_DEV = 128
PAST_DEV = 256
SINK = 4
QW = 3072
KVW = 2048
REQS = 32
TOKENS = 4096
PREFIX = 128
WINDOW = 256
N_GROUP = 4
N_REQ = 8


def draw_queries(key, part):
    values = jax.random.normal(key, (TOKENS, HEADS * HEAD), jnp.float32)
    values = jnp.clip(values, -6.0, 6.0)
    return values.astype(jnp.bfloat16)


def block_levels(own_key, extent, split, smallest, high):
    def one(position, blocks):
        draws = jax.random.uniform(jax.random.fold_in(jax.random.fold_in(own_key, 6), position), (blocks,), jnp.float32, smallest / len(split), high / len(split))
        return jnp.repeat(jnp.exp(draws), extent[position] // blocks).reshape((-1,) + (1,) * (len(extent) - position - 1))

    gain = one(*split[0])
    for cut in split[1:]:
        gain = gain * one(*cut)
    return gain


def length_profile(number_of, total, limit, skew):
    portions = [(1 << 20) // math.isqrt(grade ** skew) + 1 for grade in range(2, number_of + 1)]
    rest, counts = total - limit - (number_of - 1), [1] * (number_of - 1)
    while rest > 0:
        movable = [i for i in range(number_of - 1) if counts[i] < limit]
        whole, left = sum([portions[i] for i in movable]), rest
        for i in movable:
            more = min(limit - counts[i], max(1, left * portions[i] // whole), rest)
            counts[i] = counts[i] + more
            rest = rest - more
    return np.array([limit] + counts)


def uneven(key, count, total, limit, slope):
    if count == 2:
        one = jax.random.randint(key, (), max(1, total - limit), min(limit, total - 1) + 1)
        return jnp.stack([one, total - one])
    sizes = jnp.asarray(length_profile(count, total, limit, slope), jnp.int32)
    twos = (count - 1) // 2
    source_of, receiver = sizes[1:1 + 2 * twos:2], sizes[2:2 + 2 * twos:2]
    slack = jnp.minimum(source_of - 1, limit - receiver)
    moved = jax.random.randint(jax.random.fold_in(key, 1), (twos,), 0, 1 << 20) % (slack + 1)
    sizes = sizes.at[1:1 + 2 * twos:2].set(source_of - moved).at[2:2 + 2 * twos:2].set(receiver + moved)
    return sizes[jax.random.permutation(jax.random.fold_in(key, 2), count)]


def centred(own_key, dims, spread, limit, pieces=(), held_as=jnp.bfloat16):
    level = block_levels(own_key, dims, pieces, -0.22, 0.18) if pieces else 1.0
    drawn = jax.random.normal(own_key, dims, jnp.float32) * spread * level
    return jnp.minimum(jnp.maximum(drawn, -limit), limit).astype(held_as)


def setup_inputs(seed: int = 0) -> dict:
    keys = jax.random.split(jax.random.key(seed), 13)
    layer_input = centred(keys[0], (TOKENS, D), 1.0, 6.0, ((0, 32),))
    queries = draw_queries(jax.random.fold_in(keys[12], 71), 0)
    suffix_kv = centred(keys[2], (TOKENS, KVW), 1.0, 6.0, ((0, 32),))
    past_kv = centred(keys[3], (REQS * PAST_DEV, KVW), 1.0, 6.0, ((0, 32),))
    prefix_kv = centred(keys[4], (N_GROUP * PREFIX, KVW), 1.0, 6.0, ((0, 32),))
    suffix_len = uneven(keys[5], REQS, 3 * TOK_DEV * REQS // 4, TOK_DEV, 2).astype(jnp.int32)
    past_len = uneven(keys[6], REQS, PAST_DEV * REQS // 2, PAST_DEV, 2).astype(jnp.int32)
    out_weight = centred(keys[7], (QW, D), QW ** -0.5, 0.109375, ((0, 4),))
    norm_gain = jnp.clip(1.0 + 0.1 * jax.random.normal(keys[8], (D,), jnp.float32), 0.5, 1.5).astype(jnp.bfloat16)
    gate_weight = centred(keys[9], (D, FF), D ** -0.5, 0.109375, ((1, 8),))
    up_weight = centred(keys[10], (D, FF), D ** -0.5, 0.109375, ((1, 8),))
    down_weight = centred(keys[11], (FF, D), FF ** -0.5, 0.0625, ((0, 8),))
    return dict(layer_input=layer_input, queries=queries, suffix_kv=suffix_kv, past_kv=past_kv, prefix_kv=prefix_kv, suffix_len=suffix_len, past_len=past_len, out_weight=out_weight, norm_gain=norm_gain, gate_weight=gate_weight, up_weight=up_weight, down_weight=down_weight)


def attend(query_rows, key_rows, key_pos, key_valid, query_pos):
    count = query_rows.shape[0]
    total_keys = key_rows.shape[0]
    ratio = HEADS // KV_HEADS
    query_heads = query_rows.astype(jnp.float32).reshape(count, KV_HEADS, ratio, HEAD)
    key_heads = key_rows[:, :KV_HEADS * HEAD].astype(jnp.float32).reshape(total_keys, KV_HEADS, HEAD)
    value_heads = key_rows[:, KV_HEADS * HEAD:].astype(jnp.float32).reshape(total_keys, KV_HEADS, HEAD)
    scores = jnp.einsum('skgh,nkh->kgsn', query_heads, key_heads) * HEAD ** (-0.5)
    near = query_pos[:, None] - key_pos[None, :] < WINDOW
    allowed = key_valid[None, :] & (key_pos[None, :] <= query_pos[:, None]) & ((key_pos[None, :] < SINK) | near)
    scores = jnp.where(allowed, scores, -1e+30)
    largest = lax.optimization_barrier(jnp.max(scores, axis=-1, keepdims=True))
    expo = jnp.where(allowed, jnp.exp(scores - largest), 0.0)
    denom = lax.optimization_barrier(jnp.sum(expo, axis=-1))
    probs = lax.optimization_barrier(expo.astype(jnp.bfloat16)).astype(jnp.float32)
    summed = jnp.einsum('kgsn,nkh->kgsh', probs, value_heads)
    result = summed / denom[..., None]
    return result.transpose(2, 0, 1, 3).reshape(count, HEADS * HEAD).astype(jnp.bfloat16)

def reference(layer_input, queries, suffix_kv, past_kv, prefix_kv, suffix_len, past_len, out_weight, norm_gain, gate_weight, up_weight, down_weight):

    def one_request(index):
        group_index = index // N_REQ
        query_rows = lax.dynamic_slice_in_dim(queries, index * TOK_DEV, TOK_DEV, 0)
        own_rows = lax.dynamic_slice_in_dim(suffix_kv, index * TOK_DEV, TOK_DEV, 0)
        past_rows = lax.dynamic_slice_in_dim(past_kv, index * PAST_DEV, PAST_DEV, 0)
        prefix_rows = lax.dynamic_slice_in_dim(prefix_kv, group_index * PREFIX, PREFIX, 0)
        past_count = past_len[index]
        offsets = jnp.arange(TOK_DEV, dtype=jnp.int32)
        query_pos = PREFIX + past_count + offsets
        key_rows = jnp.concatenate([prefix_rows, past_rows, own_rows], axis=0)
        key_pos = jnp.concatenate([jnp.arange(PREFIX, dtype=jnp.int32), PREFIX + jnp.arange(PAST_DEV, dtype=jnp.int32), query_pos])
        key_valid = jnp.concatenate([jnp.ones((PREFIX,), bool), jnp.arange(PAST_DEV, dtype=jnp.int32) < past_count, jnp.ones((TOK_DEV,), bool)])
        return attend(query_rows, key_rows, key_pos, key_valid, query_pos)
    attended = lax.map(one_request, jnp.arange(REQS, dtype=jnp.int32)).reshape(TOKENS, HEADS * HEAD)
    mixed = layer_input.astype(jnp.float32) + jnp.dot(attended, out_weight, preferred_element_type=jnp.float32)
    scale = lax.rsqrt(lax.optimization_barrier(jnp.mean(mixed * mixed, axis=-1, keepdims=True)) + 1e-05)
    normed = (mixed * scale * norm_gain.astype(jnp.float32)).astype(jnp.bfloat16)
    down_blocks = down_weight.astype(jnp.float32).reshape(N_REQ, FF // N_REQ, D)

    def feed_block(rows):
        gate = jnp.dot(rows, gate_weight, preferred_element_type=jnp.float32)
        upper = jnp.dot(rows, up_weight, preferred_element_type=jnp.float32)
        hidden = (jax.nn.silu(gate) * upper).astype(jnp.bfloat16)
        shards = hidden.reshape(rows.shape[0], N_REQ, FF // N_REQ).astype(jnp.float32)
        parts = jnp.einsum('tkf,kfd->ktd', shards, down_blocks)
        parts = lax.optimization_barrier(parts.astype(jnp.bfloat16)).astype(jnp.float32)
        return lax.optimization_barrier(jnp.sum(parts, axis=0))
    feed = lax.map(feed_block, normed.reshape(REQS, TOK_DEV, D)).reshape(TOKENS, D)
    live = (jnp.arange(TOK_DEV, dtype=jnp.int32)[None, :] < suffix_len[:, None]).reshape(TOKENS)
    return jnp.where(live[:, None], mixed + feed, 0.0).astype(jnp.bfloat16)
```

```python
import functools

import jax
import jax.numpy as jnp
from jax import lax
from jax.experimental import pallas as pl
from jax.experimental.pallas import tpu as pltpu
from jax.sharding import PartitionSpec as P

HEADS = 24
KV_HEADS = 8
HEAD = 128
SINK = 4
MESH = pl.DeviceIdType.MESH
CHUNKS = 2


def absorb(state, query_heads, key_rows, key_pos, key_valid, query_pos, window):
    maxima, totals, sums = state
    count = key_rows.shape[0]
    key_heads = key_rows[:, : KV_HEADS * HEAD].reshape(count, KV_HEADS, HEAD)
    value_heads = key_rows[:, KV_HEADS * HEAD :].reshape(count, KV_HEADS, HEAD)
    scores = jnp.einsum(
        "skgh,nkh->kgsn", query_heads, key_heads, preferred_element_type=jnp.float32
    ) * HEAD ** (-0.5)
    near = query_pos[:, None] - key_pos[None, :] < window
    allowed = (
        key_valid[None, :]
        & (key_pos[None, :] <= query_pos[:, None])
        & ((key_pos[None, :] < SINK) | near)
    )
    scores = jnp.where(allowed, scores, -1e30)
    new_max = jnp.maximum(maxima, jnp.max(scores, axis=-1))
    expo = jnp.where(allowed, jnp.exp(scores - new_max[..., None]), 0.0)
    factor = jnp.exp(maxima - new_max)
    totals = totals * factor + jnp.sum(expo, axis=-1)
    sums = sums * factor[..., None] + jnp.einsum(
        "kgsn,nkh->kgsh", expo.astype(jnp.bfloat16), value_heads, preferred_element_type=jnp.float32
    )
    return (new_max, totals, sums)


def shards(
    layer_input,
    queries,
    suffix_kv,
    past_kv,
    prefix_kv,
    suffix_len,
    past_len,
    out_weight,
    norm_gain,
    gate_weight,
    up_weight,
    down_weight,
):
    rows_here = queries.shape[0]
    past_slots = past_kv.shape[0]
    prefix_total = prefix_kv.shape[0] * lax.axis_size("req")
    window = prefix_total + past_slots // 2
    past_count = past_len[0]
    offsets = jnp.arange(rows_here, dtype=jnp.int32)
    query_pos = prefix_total + past_count + offsets
    ratio = HEADS // KV_HEADS
    query_heads = queries.reshape(rows_here, KV_HEADS, ratio, HEAD)
    state = (
        jnp.full((KV_HEADS, ratio, rows_here), -1e30, jnp.float32),
        jnp.zeros((KV_HEADS, ratio, rows_here), jnp.float32),
        jnp.zeros((KV_HEADS, ratio, rows_here, HEAD), jnp.float32),
    )
    local_rows = jnp.concatenate([past_kv, suffix_kv], axis=0)
    local_pos = jnp.concatenate([prefix_total + jnp.arange(past_slots, dtype=jnp.int32), query_pos])
    local_valid = jnp.concatenate(
        [jnp.arange(past_slots, dtype=jnp.int32) < past_count, jnp.ones((rows_here,), bool)]
    )
    state = absorb(state, query_heads, local_rows, local_pos, local_valid, query_pos, window)
    piece = lax.all_gather(prefix_kv, "req", axis=0, tiled=True)
    count = piece.shape[0]
    positions = jnp.arange(count, dtype=jnp.int32)
    maxima, totals, sums = absorb(
        state, query_heads, piece, positions, jnp.ones((count,), bool), query_pos, window
    )
    attended = (
        (sums / totals[..., None])
        .transpose(2, 0, 1, 3)
        .reshape(rows_here, HEADS * HEAD)
        .astype(jnp.bfloat16)
    )
    blocks = lax.axis_size("group")
    split_rows = attended.reshape(rows_here, blocks, attended.shape[1] // blocks)
    received = lax.all_to_all(split_rows, "group", split_axis=1, concat_axis=0, tiled=True)
    received = received.reshape(blocks * rows_here, attended.shape[1] // blocks)
    picked = received
    projected = lax.psum_scatter(
        jnp.dot(picked, out_weight, preferred_element_type=jnp.float32).astype(jnp.bfloat16),
        "group",
        scatter_dimension=0,
        tiled=True,
    ).astype(jnp.float32)
    mixed = layer_input.astype(jnp.float32) + projected
    scale = lax.rsqrt(jnp.mean(mixed * mixed, axis=-1, keepdims=True) + 1e-05)
    normed = (mixed * scale * norm_gain.astype(jnp.float32)).astype(jnp.bfloat16)
    gathered = lax.all_gather(normed, "req", axis=0, tiled=True)
    picked = gathered
    gate = jnp.dot(picked, gate_weight, preferred_element_type=jnp.float32)
    upper = jnp.dot(picked, up_weight, preferred_element_type=jnp.float32)
    hidden = (jax.nn.silu(gate) * upper).astype(jnp.bfloat16)
    feed = lax.psum_scatter(
        jnp.dot(hidden, down_weight, preferred_element_type=jnp.float32).astype(jnp.bfloat16),
        "req",
        scatter_dimension=0,
        tiled=True,
    ).astype(jnp.float32)
    live = offsets < suffix_len[0]
    return jnp.where(live[:, None], mixed + feed, 0.0).astype(jnp.bfloat16)


def layer_kernel(
    n_group,
    input_hbm,
    query_hbm,
    suffix_hbm,
    past_hbm,
    prefix_hbm,
    suffix_len,
    past_len,
    outw_hbm,
    gain_ref,
    gate_hbm,
    up_hbm,
    down_hbm,
    out_ref,
    query,
    rows_kv,
    bias,
    residual,
    out_w,
    attended,
    normed,
    gate_w,
    up_w,
    down_w,
    hidden,
    row_scale,
    parts,
    sums,
    first,
    second,
    local_sem,
    send_sem,
    recv_sem,
    z_send,
    z_recv,
):
    n_req = 8
    z = lax.axis_index("group")
    r = lax.axis_index("req")
    core, x, y = r % 2, (r // 2) % 2, r // 4

    def flip(mask):
        c2 = 1 - core if mask & 1 else core
        x2 = 1 - x if mask & 2 else x
        y2 = 1 - y if mask & 4 else y
        return y2 * 4 + x2 * 2 + c2

    tokens, width = query.shape
    rows = tokens // CHUNKS
    past_slots = past_hbm.shape[0]
    own_prefix = prefix_hbm.shape[0]
    prefix = own_prefix * n_req
    window = prefix + past_slots // 2
    depth = outw_hbm.shape[0]
    cols = width // n_req
    half = width // 2
    kv_cols = KV_HEADS * HEAD
    keys = prefix + past_slots + tokens

    def col_slice(owner):
        return pl.ds(pl.multiple_of(owner * cols, 128), cols)

    def row_slice(owner, count):
        return pl.ds(pl.multiple_of(owner * count, 16), count)

    used = [0]
    started = []

    def reserve(count):
        base = used[0]
        used[0] += count
        return base

    def remote(src, dst, index, device):
        return pltpu.make_async_remote_copy(
            src_ref=src,
            dst_ref=dst,
            send_sem=send_sem.at[index],
            recv_sem=recv_sem.at[index],
            device_id={"req": device},
            device_id_type=MESH,
        )

    def begin(copy):
        copy.start()
        started.append(copy)

    def local(src, dst, index):
        copy = pltpu.make_async_copy(src, dst, local_sem.at[index])
        copy.start()
        return copy

    small = [
        local(query_hbm, query, 0),
        local(past_hbm, rows_kv.at[pl.ds(prefix, past_slots)], 1),
        local(suffix_hbm, rows_kv.at[pl.ds(prefix + past_slots, tokens)], 2),
        local(prefix_hbm, rows_kv.at[row_slice(r, own_prefix)], 3),
    ]
    own_w = local(outw_hbm.at[:, col_slice(r)], out_w.at[row_slice(z, depth)], 4)
    own_x = local(input_hbm.at[:, col_slice(r)], residual.at[r], 5)

    barrier = pltpu.get_barrier_semaphore()
    for mask in range(1, n_req):
        pl.semaphore_signal(barrier, inc=1, device_id={"req": flip(mask)}, device_id_type=MESH)
    has_left, has_right = z > 0, z < n_group - 1

    @pl.when(has_left)
    def _():
        pl.semaphore_signal(barrier, inc=1, device_id={"group": z - 1}, device_id_type=MESH)

    @pl.when(has_right)
    def _():
        pl.semaphore_signal(barrier, inc=1, device_id={"group": z + 1}, device_id_type=MESH)

    peers = n_req - 1 + jnp.where(has_left, 1, 0) + jnp.where(has_right, 1, 0)
    pl.semaphore_wait(barrier, peers)

    prefix_copies = []
    base = reserve(n_req - 1)
    for mask in range(1, n_req):
        copy = remote(prefix_hbm, rows_kv.at[row_slice(r, own_prefix)], base + mask - 1, flip(mask))
        begin(copy)
        prefix_copies.append(copy)

    def z_copy(direction, step):
        block = z - (step - 1) if direction == 0 else z + (step - 1)
        where = out_w.at[row_slice(block, depth)]
        src = outw_hbm.at[:, col_slice(r)] if step == 1 else where
        return pltpu.make_async_remote_copy(
            src_ref=src,
            dst_ref=where,
            send_sem=z_send.at[direction, step - 1],
            recv_sem=z_recv.at[direction, step - 1],
            device_id={"group": z + 1 if direction == 0 else z - 1},
            device_id_type=MESH,
        )

    def z_sends(direction, step):
        if direction == 0:
            return (z - (step - 1) >= 0) & has_right
        return (z + (step - 1) <= n_group - 1) & has_left

    def z_gets(direction, step):
        return z - step >= 0 if direction == 0 else z + step <= n_group - 1

    def z_arrived(direction, step):
        block = z - step if direction == 0 else z + step
        where = out_w.at[row_slice(block, depth)]
        pltpu.make_async_remote_copy(
            src_ref=where,
            dst_ref=where,
            send_sem=z_send.at[direction, step - 1],
            recv_sem=z_recv.at[direction, step - 1],
            device_id={"req": flip(1)},
            device_id_type=MESH,
        ).wait_recv()

    def z_step(step):
        for direction in (0, 1):
            if step > 1:

                @pl.when(z_gets(direction, step - 1))
                def _():
                    z_arrived(direction, step - 1)

            if step < n_group:

                @pl.when(z_sends(direction, step))
                def _():
                    z_copy(direction, step).start()

    z_step(1)

    input_copies = []
    base = reserve(n_req - 1)
    for mask in range(1, n_req):
        other = flip(mask)
        copy = remote(input_hbm.at[:, col_slice(other)], residual.at[r], base + mask - 1, other)
        begin(copy)
        input_copies.append(copy)

    weights = [
        local(gate_hbm, gate_w, 6),
        local(up_hbm, up_w, 7),
        local(down_hbm, down_w, 8),
    ]

    ratio = HEADS // KV_HEADS
    past_count = past_len[0]
    for chunk in range(CHUNKS):
        key = lax.broadcasted_iota(jnp.int32, (rows, keys), 1)
        token = lax.broadcasted_iota(jnp.int32, (rows, keys), 0) + chunk * rows
        query_pos = prefix + past_count + token
        key_pos = jnp.where(key < prefix + past_slots, key, key - past_slots + past_count)
        valid = (key < prefix + past_count) | (key >= prefix + past_slots)
        allowed = valid & (key_pos <= query_pos) & ((key_pos < SINK) | (query_pos - key_pos < window))
        term = jnp.where(allowed, 0.0, -1e30)
        for head in range(ratio):
            bias[chunk, pl.ds(head * rows, rows), :] = term

    for copy in small:
        copy.wait()
    for copy in prefix_copies:
        copy.wait_recv()

    def attend(chunk, group):
        lanes = pl.multiple_of(group * (ratio * HEAD), 128)
        mine = jnp.concatenate(
            [
                query[pl.ds(chunk * rows, rows), pl.ds(lanes + head * HEAD, HEAD)]
                for head in range(ratio)
            ],
            axis=0,
        )
        keys_here = rows_kv[:, pl.ds(pl.multiple_of(group * HEAD, 128), HEAD)]
        values = rows_kv[:, pl.ds(pl.multiple_of(kv_cols + group * HEAD, 128), HEAD)]
        scores = lax.dot_general(
            mine, keys_here, (((1,), (1,)), ((), ())), preferred_element_type=jnp.float32
        )
        scores = scores * HEAD ** (-0.5) + bias[chunk]
        expo = jnp.exp(scores - jnp.max(scores, axis=-1, keepdims=True))
        denom = jnp.sum(expo, axis=-1, keepdims=True)
        result = jnp.dot(expo.astype(jnp.bfloat16), values, preferred_element_type=jnp.float32) / denom
        result = result.astype(jnp.bfloat16)
        for head in range(ratio):
            attended[chunk, row_slice(r, rows), pl.ds(lanes + head * HEAD, HEAD)] = result[
                head * rows : (head + 1) * rows
            ]

    class Gather:
        def __init__(self, region):
            self.region = region
            base = reserve(14)
            X, Y, S = flip(2), flip(4), flip(1)
            plan = [
                (r, 0, X), (r, 1, Y), (r, 1, X), (r, 0, Y),
                (X, 0, Y), (Y, 1, X),
                (r, 0, S), (r, 1, S),
                (X, 0, S), (Y, 1, S), (X, 1, S), (Y, 0, S),
                (flip(6), 0, S), (flip(6), 1, S),
            ]
            self.copies = [
                remote(region(owner, rail), region(owner, rail), base + i, device)
                for i, (owner, rail, device) in enumerate(plan)
            ]

        def go(self, *which):
            for i in which:
                begin(self.copies[i])

        def got(self, *which):
            for i in which:
                self.copies[i].wait_recv()

        def forward(self):
            self.got(0)
            self.go(4, 8)
            self.got(1)
            self.go(5, 9)
            self.got(2)
            self.go(10)
            self.got(3)
            self.go(11)

        def relay(self):
            self.got(4)
            self.go(12)
            self.got(5)
            self.go(13)

        def finish(self):
            self.got(6, 7, 8, 9, 10, 11, 12, 13)

    def attended_region(chunk):
        return lambda owner, rail: attended.at[chunk, row_slice(owner, rows), pl.ds(rail * half, half)]

    def normed_region(chunk):
        band = n_req * rows // 2
        return lambda owner, rail: normed.at[chunk, pl.ds(rail * band, band), col_slice(owner)]

    heads_gather = [Gather(attended_region(chunk)) for chunk in range(CHUNKS)]
    token_gather = [Gather(normed_region(chunk)) for chunk in range(CHUNKS)]

    for chunk in range(CHUNKS):

        @pl.loop(0, KV_HEADS // 2)
        def _(group):
            attend(chunk, group)

        heads_gather[chunk].go(0, 3, 6)

        @pl.loop(KV_HEADS // 2, KV_HEADS)
        def _(group):
            attend(chunk, group)

        heads_gather[chunk].go(1, 2, 7)

    z_step(2)
    heads_gather[0].forward()
    heads_gather[0].relay()
    z_step(3)
    heads_gather[1].forward()
    heads_gather[1].relay()
    for copy in input_copies:
        copy.wait_recv()
    own_x.wait()
    own_w.wait()
    heads_gather[0].finish()
    heads_gather[1].finish()
    z_step(4)

    gain_here = gain_ref[:, col_slice(r)].astype(jnp.float32)

    def project(chunk):
        total = jnp.dot(attended[chunk], out_w[...], preferred_element_type=jnp.float32)
        total = total + residual[:, pl.ds(chunk * rows, rows), :].astype(jnp.float32).reshape(
            n_req * rows, cols
        )
        normed[chunk, :, col_slice(r)] = (total * gain_here).astype(jnp.bfloat16)
        token_gather[chunk].go(0, 1, 2, 3, 6, 7)

    def norms(chunk):
        inverse = 1.0 / gain_ref[...].astype(jnp.float32)

        @pl.loop(0, n_req)
        def _(block):
            where = row_slice(block, rows)
            values = normed[chunk, where, :].astype(jnp.float32) * inverse
            mean = jnp.sum(values * values, axis=-1, keepdims=True) / width
            row_scale[where, :] = lax.rsqrt(mean + 1e-05)

    tile = 256

    def widen(chunk, start, stop):
        @pl.loop(start, stop)
        def _(i):
            lanes = pl.ds(pl.multiple_of(i * tile, 128), tile)
            gate = jnp.dot(normed[chunk], gate_w[:, lanes], preferred_element_type=jnp.float32)
            upper = jnp.dot(normed[chunk], up_w[:, lanes], preferred_element_type=jnp.float32)
            scale = row_scale[...]
            gate = gate * scale
            hidden[:, lanes] = (gate / (1.0 + jnp.exp(-gate)) * (upper * scale)).astype(jnp.bfloat16)

    def narrow(chunk, rail):
        step = 512

        @pl.loop(0, half // step)
        def _(i):
            lanes = pl.ds(pl.multiple_of(rail * half + i * step, 128), step)
            part = jnp.dot(hidden[...], down_w[:, lanes], preferred_element_type=jnp.float32)
            parts[chunk, :, :, :, :, lanes] = part.astype(jnp.bfloat16).reshape(2, 2, 2, rows, step)

    def rail_cols(rail):
        return pl.ds(rail * half, half)

    def scatter_copies(chunk, rail):
        lanes = rail_cols(rail)
        base = reserve(3)
        to_core = remote(
            parts.at[chunk, :, :, 1 - core, :, lanes], sums.at[chunk, :, :, :, lanes], base, flip(1)
        )
        if rail == 0:
            far = remote(sums.at[chunk, 1 - y, :, :, lanes], first.at[chunk, rail], base + 1, flip(4))
            near = remote(sums.at[chunk, y, 1 - x, :, lanes], second.at[chunk, rail], base + 2, flip(2))
        else:
            far = remote(sums.at[chunk, :, 1 - x, :, lanes], first.at[chunk, rail], base + 1, flip(2))
            near = remote(sums.at[chunk, 1 - y, x, :, lanes], second.at[chunk, rail], base + 2, flip(4))
        return to_core, far, near

    scatter = [[scatter_copies(chunk, rail) for rail in (0, 1)] for chunk in range(CHUNKS)]

    def f32(value):
        return value.astype(jnp.float32)

    def scatter_core(chunk, rail):
        begin(scatter[chunk][rail][0])

    def scatter_far(chunk, rail):
        lanes = rail_cols(rail)
        scatter[chunk][rail][0].wait_recv()
        for a in (0, 1):
            for b in (0, 1):
                sums[chunk, a, b, :, lanes] = (
                    f32(sums[chunk, a, b, :, lanes]) + f32(parts[chunk, a, b, core, :, lanes])
                ).astype(jnp.bfloat16)
        begin(scatter[chunk][rail][1])

    def scatter_near(chunk, rail):
        lanes = rail_cols(rail)
        scatter[chunk][rail][1].wait_recv()
        for i in (0, 1):
            a, b = (y, i) if rail == 0 else (i, x)
            sums[chunk, a, b, :, lanes] = (
                f32(sums[chunk, a, b, :, lanes]) + f32(first[chunk, rail, i])
            ).astype(jnp.bfloat16)
        begin(scatter[chunk][rail][2])

    def scatter_end(chunk, rail):
        lanes = rail_cols(rail)
        scatter[chunk][rail][2].wait_recv()
        feed = f32(sums[chunk, y, x, :, lanes]) + f32(second[chunk, rail])
        mixed = f32(normed[chunk, row_slice(r, rows), lanes]) / f32(gain_ref[:, lanes])
        token = lax.broadcasted_iota(jnp.int32, (rows, half), 0) + chunk * rows
        out_ref[pl.ds(chunk * rows, rows), lanes] = jnp.where(
            token < suffix_len[0], mixed + feed, 0.0
        ).astype(jnp.bfloat16)

    tiles = gate_w.shape[1] // tile
    project(0)
    project(1)
    token_gather[0].forward()
    token_gather[0].relay()
    token_gather[0].finish()
    norms(0)
    for copy in weights:
        copy.wait()
    widen(0, 0, tiles // 2)
    token_gather[1].forward()
    widen(0, tiles // 2, tiles)
    token_gather[1].relay()
    narrow(0, 0)
    scatter_core(0, 0)
    narrow(0, 1)
    scatter_core(0, 1)
    scatter_far(0, 0)
    token_gather[1].finish()
    norms(1)
    scatter_far(0, 1)
    widen(1, 0, tiles // 2)
    widen(1, tiles // 2, tiles)
    scatter_near(0, 0)
    scatter_near(0, 1)
    narrow(1, 0)
    scatter_core(1, 0)
    narrow(1, 1)
    scatter_core(1, 1)
    scatter_far(1, 0)
    scatter_far(1, 1)
    scatter_end(0, 0)
    scatter_end(0, 1)
    scatter_near(1, 0)
    scatter_near(1, 1)
    scatter_end(1, 0)
    scatter_end(1, 1)

    for copy in started:
        copy.wait_send()
    for step in range(1, n_group):
        for direction in (0, 1):

            @pl.when(z_sends(direction, step))
            def _():
                z_copy(direction, step).wait_send()


def fused(n_group, *args):
    (
        layer_input,
        queries,
        suffix_kv,
        past_kv,
        prefix_kv,
        suffix_len,
        past_len,
        out_weight,
        norm_gain,
        gate_weight,
        up_weight,
        down_weight,
    ) = args
    n_req = 8
    tokens, width = queries.shape
    rows = tokens // CHUNKS
    cols = width // n_req
    ff = gate_weight.shape[1]
    keys = n_req * prefix_kv.shape[0] + past_kv.shape[0] + tokens
    half = width // 2
    bf16, f32 = jnp.bfloat16, jnp.float32
    hbm = pl.BlockSpec(memory_space=pl.ANY)
    smem = pl.BlockSpec(memory_space=pltpu.SMEM)
    vmem = pl.BlockSpec(memory_space=pltpu.VMEM)
    n_copies = 2 * (n_req - 1) + 14 * 2 * CHUNKS + 6 * CHUNKS
    return pl.pallas_call(
        functools.partial(layer_kernel, n_group),
        out_shape=jax.ShapeDtypeStruct((tokens, width), bf16),
        in_specs=[hbm, hbm, hbm, hbm, hbm, smem, smem, hbm, vmem, hbm, hbm, hbm],
        out_specs=vmem,
        scratch_shapes=[
            pltpu.VMEM((tokens, width), bf16),
            pltpu.VMEM((keys, suffix_kv.shape[1]), bf16),
            pltpu.VMEM((CHUNKS, HEADS // KV_HEADS * rows, keys), f32),
            pltpu.VMEM((n_req, tokens, cols), bf16),
            pltpu.VMEM((n_group * out_weight.shape[0], cols), bf16),
            pltpu.VMEM((CHUNKS, n_req * rows, width), bf16),
            pltpu.VMEM((CHUNKS, n_req * rows, width), bf16),
            pltpu.VMEM((width, ff), bf16),
            pltpu.VMEM((width, ff), bf16),
            pltpu.VMEM((ff, width), bf16),
            pltpu.VMEM((n_req * rows, ff), bf16),
            pltpu.VMEM((n_req * rows, 1), f32),
            pltpu.VMEM((CHUNKS, 2, 2, 2, rows, width), bf16),
            pltpu.VMEM((CHUNKS, 2, 2, rows, width), bf16),
            pltpu.VMEM((CHUNKS, 2, 2, rows, half), bf16),
            pltpu.VMEM((CHUNKS, 2, rows, half), bf16),
            pltpu.SemaphoreType.DMA((9,)),
            pltpu.SemaphoreType.DMA((n_copies,)),
            pltpu.SemaphoreType.DMA((n_copies,)),
            pltpu.SemaphoreType.DMA((2, n_group - 1)),
            pltpu.SemaphoreType.DMA((2, n_group - 1)),
        ],
        compiler_params=pltpu.CompilerParams(
            collective_id=0, has_side_effects=True, vmem_limit_bytes=62 * 2**20
        ),
    )(
        layer_input,
        queries,
        suffix_kv,
        past_kv,
        prefix_kv,
        suffix_len,
        past_len,
        out_weight,
        norm_gain.reshape(1, width),
        gate_weight,
        up_weight,
        down_weight,
    )


def solution(mesh):
    in_specs = (
        P(("group", "req"), None),
        P(("group", "req"), None),
        P(("group", "req"), None),
        P(("group", "req"), None),
        P(("group", "req"), None),
        P(("group", "req")),
        P(("group", "req")),
        P("group", None),
        P(),
        P(None, "req"),
        P(None, "req"),
        P("req", None),
    )
    out_specs = P(("group", "req"), None)
    body = functools.partial(fused, mesh.shape["group"]) if dict(mesh.shape) == {"group": 4, "req": 8} else shards
    return jax.shard_map(body, mesh=mesh, in_specs=in_specs, out_specs=out_specs, check_vma=False)
```

```python
import functools

import jax
import jax.numpy as jnp
from jax import lax
from jax.experimental import pallas as pl
from jax.experimental.pallas import tpu as pltpu
from jax.sharding import PartitionSpec as P

HEADS = 24
KV_HEADS = 8
HEAD = 128
SINK = 4
MESH = pl.DeviceIdType.MESH
CHUNKS = 2
Z_PARTS = 2
PIECES = 4


def absorb(state, query_heads, key_rows, key_pos, key_valid, query_pos, window):
    maxima, totals, sums = state
    count = key_rows.shape[0]
    key_heads = key_rows[:, : KV_HEADS * HEAD].reshape(count, KV_HEADS, HEAD)
    value_heads = key_rows[:, KV_HEADS * HEAD :].reshape(count, KV_HEADS, HEAD)
    scores = jnp.einsum(
        "skgh,nkh->kgsn", query_heads, key_heads, preferred_element_type=jnp.float32
    ) * HEAD ** (-0.5)
    near = query_pos[:, None] - key_pos[None, :] < window
    allowed = (
        key_valid[None, :]
        & (key_pos[None, :] <= query_pos[:, None])
        & ((key_pos[None, :] < SINK) | near)
    )
    scores = jnp.where(allowed, scores, -1e30)
    new_max = jnp.maximum(maxima, jnp.max(scores, axis=-1))
    expo = jnp.where(allowed, jnp.exp(scores - new_max[..., None]), 0.0)
    factor = jnp.exp(maxima - new_max)
    totals = totals * factor + jnp.sum(expo, axis=-1)
    sums = sums * factor[..., None] + jnp.einsum(
        "kgsn,nkh->kgsh", expo.astype(jnp.bfloat16), value_heads, preferred_element_type=jnp.float32
    )
    return (new_max, totals, sums)


def shards(
    layer_input,
    queries,
    suffix_kv,
    past_kv,
    prefix_kv,
    suffix_len,
    past_len,
    out_weight,
    norm_gain,
    gate_weight,
    up_weight,
    down_weight,
):
    rows_here = queries.shape[0]
    past_slots = past_kv.shape[0]
    prefix_total = prefix_kv.shape[0] * lax.axis_size("req")
    window = prefix_total + past_slots // 2
    past_count = past_len[0]
    offsets = jnp.arange(rows_here, dtype=jnp.int32)
    query_pos = prefix_total + past_count + offsets
    ratio = HEADS // KV_HEADS
    query_heads = queries.reshape(rows_here, KV_HEADS, ratio, HEAD)
    state = (
        jnp.full((KV_HEADS, ratio, rows_here), -1e30, jnp.float32),
        jnp.zeros((KV_HEADS, ratio, rows_here), jnp.float32),
        jnp.zeros((KV_HEADS, ratio, rows_here, HEAD), jnp.float32),
    )
    local_rows = jnp.concatenate([past_kv, suffix_kv], axis=0)
    local_pos = jnp.concatenate([prefix_total + jnp.arange(past_slots, dtype=jnp.int32), query_pos])
    local_valid = jnp.concatenate(
        [jnp.arange(past_slots, dtype=jnp.int32) < past_count, jnp.ones((rows_here,), bool)]
    )
    state = absorb(state, query_heads, local_rows, local_pos, local_valid, query_pos, window)
    piece = lax.all_gather(prefix_kv, "req", axis=0, tiled=True)
    count = piece.shape[0]
    positions = jnp.arange(count, dtype=jnp.int32)
    maxima, totals, sums = absorb(
        state, query_heads, piece, positions, jnp.ones((count,), bool), query_pos, window
    )
    attended = (
        (sums / totals[..., None])
        .transpose(2, 0, 1, 3)
        .reshape(rows_here, HEADS * HEAD)
        .astype(jnp.bfloat16)
    )
    blocks = lax.axis_size("group")
    split_rows = attended.reshape(rows_here, blocks, attended.shape[1] // blocks)
    received = lax.all_to_all(split_rows, "group", split_axis=1, concat_axis=0, tiled=True)
    received = received.reshape(blocks * rows_here, attended.shape[1] // blocks)
    picked = received
    projected = lax.psum_scatter(
        jnp.dot(picked, out_weight, preferred_element_type=jnp.float32).astype(jnp.bfloat16),
        "group",
        scatter_dimension=0,
        tiled=True,
    ).astype(jnp.float32)
    mixed = layer_input.astype(jnp.float32) + projected
    scale = lax.rsqrt(jnp.mean(mixed * mixed, axis=-1, keepdims=True) + 1e-05)
    normed = (mixed * scale * norm_gain.astype(jnp.float32)).astype(jnp.bfloat16)
    gathered = lax.all_gather(normed, "req", axis=0, tiled=True)
    picked = gathered
    gate = jnp.dot(picked, gate_weight, preferred_element_type=jnp.float32)
    upper = jnp.dot(picked, up_weight, preferred_element_type=jnp.float32)
    hidden = (jax.nn.silu(gate) * upper).astype(jnp.bfloat16)
    feed = lax.psum_scatter(
        jnp.dot(hidden, down_weight, preferred_element_type=jnp.float32).astype(jnp.bfloat16),
        "req",
        scatter_dimension=0,
        tiled=True,
    ).astype(jnp.float32)
    live = offsets < suffix_len[0]
    return jnp.where(live[:, None], mixed + feed, 0.0).astype(jnp.bfloat16)


def layer_kernel(
    n_group,
    input_hbm,
    query_hbm,
    suffix_hbm,
    past_hbm,
    prefix_hbm,
    suffix_len,
    past_len,
    outw_hbm,
    gain_ref,
    gate_hbm,
    up_hbm,
    down_hbm,
    out_ref,
    query,
    rows_kv,
    bias,
    residual,
    out_w,
    attended,
    normed,
    gate_w,
    up_w,
    down_w,
    hidden,
    row_scale,
    parts,
    sums,
    first,
    second,
    local_sem,
    send_sem,
    recv_sem,
    z_send,
    z_recv,
    gain,
):
    n_req = 8
    z = lax.axis_index("group")
    r = lax.axis_index("req")
    core, x, y = r % 2, (r // 2) % 2, r // 4

    def flip(mask):
        c2 = 1 - core if mask & 1 else core
        x2 = 1 - x if mask & 2 else x
        y2 = 1 - y if mask & 4 else y
        return y2 * 4 + x2 * 2 + c2

    tokens, width = query.shape
    rows = tokens // CHUNKS
    past_slots = past_hbm.shape[0]
    own_prefix = prefix_hbm.shape[0]
    prefix = own_prefix * n_req
    window = prefix + past_slots // 2
    depth = outw_hbm.shape[0]
    cols = width // n_req
    half = width // 2
    kv_cols = KV_HEADS * HEAD
    keys = prefix + past_slots + tokens

    def col_slice(owner):
        return pl.ds(pl.multiple_of(owner * cols, 128), cols)

    def row_slice(owner, count):
        return pl.ds(pl.multiple_of(owner * count, 16), count)

    used = [0]
    started = []

    def reserve(count):
        base = used[0]
        used[0] += count
        return base

    def remote(src, dst, index, device):
        return pltpu.make_async_remote_copy(
            src_ref=src,
            dst_ref=dst,
            send_sem=send_sem.at[index],
            recv_sem=recv_sem.at[index],
            device_id={"req": device},
            device_id_type=MESH,
        )

    def begin(copy):
        copy.start()
        started.append(copy)

    def local(src, dst, index):
        copy = pltpu.make_async_copy(src, dst, local_sem.at[index])
        copy.start()
        return copy

    small = [
        local(query_hbm, query, 0),
        local(past_hbm, rows_kv.at[pl.ds(prefix, past_slots)], 1),
        local(suffix_hbm, rows_kv.at[pl.ds(prefix + past_slots, tokens)], 2),
        local(prefix_hbm, rows_kv.at[row_slice(r, own_prefix)], 3),
    ]
    own_w = local(outw_hbm.at[:, col_slice(r)], out_w.at[row_slice(z, depth)], 4)
    own_x = local(input_hbm.at[:, col_slice(r)], residual.at[r], 5)

    barrier = pltpu.get_barrier_semaphore()
    for mask in range(1, n_req):
        pl.semaphore_signal(barrier, inc=1, device_id={"req": flip(mask)}, device_id_type=MESH)
    has_left, has_right = z > 0, z < n_group - 1

    @pl.when(has_left)
    def _():
        pl.semaphore_signal(barrier, inc=1, device_id={"group": z - 1}, device_id_type=MESH)

    @pl.when(has_right)
    def _():
        pl.semaphore_signal(barrier, inc=1, device_id={"group": z + 1}, device_id_type=MESH)

    peers = n_req - 1 + jnp.where(has_left, 1, 0) + jnp.where(has_right, 1, 0)
    pl.semaphore_wait(barrier, peers)

    prefix_copies = []
    base = reserve(n_req - 1)
    for mask in range(1, n_req):
        copy = remote(prefix_hbm, rows_kv.at[row_slice(r, own_prefix)], base + mask - 1, flip(mask))
        begin(copy)
        prefix_copies.append(copy)

    def z_part(block, part):
        return pl.ds(pl.multiple_of(block * depth + part * (depth // Z_PARTS), 16), depth // Z_PARTS)

    def z_copy(direction, step, part):
        block = z - (step - 1) if direction == 0 else z + (step - 1)
        where = out_w.at[z_part(block, part)]
        src = outw_hbm.at[z_part(0, part), col_slice(r)] if step == 1 else where
        return pltpu.make_async_remote_copy(
            src_ref=src,
            dst_ref=where,
            send_sem=z_send.at[direction, step - 1, part],
            recv_sem=z_recv.at[direction, step - 1, part],
            device_id={"group": z + 1 if direction == 0 else z - 1},
            device_id_type=MESH,
        )

    def z_sends(direction, step):
        if direction == 0:
            return (z - (step - 1) >= 0) & has_right
        return (z + (step - 1) <= n_group - 1) & has_left

    def z_gets(direction, step):
        return z - step >= 0 if direction == 0 else z + step <= n_group - 1

    def z_arrived(direction, step, part):
        block = z - step if direction == 0 else z + step
        where = out_w.at[z_part(block, part)]
        pltpu.make_async_remote_copy(
            src_ref=where,
            dst_ref=where,
            send_sem=z_send.at[direction, step - 1, part],
            recv_sem=z_recv.at[direction, step - 1, part],
            device_id={"req": flip(1)},
            device_id_type=MESH,
        ).wait_recv()

    def z_step(step, part):
        for direction in (0, 1):
            if step > 1:

                @pl.when(z_gets(direction, step - 1))
                def _():
                    z_arrived(direction, step - 1, part)

            if step < n_group:

                @pl.when(z_sends(direction, step))
                def _():
                    z_copy(direction, step, part).start()

    z_step(1, 0)
    z_step(1, 1)

    input_copies = []
    base = reserve(n_req - 1)
    for mask in range(1, n_req):
        other = flip(mask)
        copy = remote(input_hbm.at[:, col_slice(other)], residual.at[r], base + mask - 1, other)
        begin(copy)
        input_copies.append(copy)

    weights = [
        local(gate_hbm, gate_w, 6),
        local(up_hbm, up_w, 7),
        local(down_hbm, down_w, 8),
    ]

    gain[...] = gain_ref[...].astype(jnp.float32).reshape(gain.shape)

    ratio = HEADS // KV_HEADS
    past_count = past_len[0]
    for chunk in range(CHUNKS):
        key = lax.broadcasted_iota(jnp.int32, (rows, keys), 1)
        token = lax.broadcasted_iota(jnp.int32, (rows, keys), 0) + chunk * rows
        query_pos = prefix + past_count + token
        key_pos = jnp.where(key < prefix + past_slots, key, key - past_slots + past_count)
        valid = (key < prefix + past_count) | (key >= prefix + past_slots)
        allowed = valid & (key_pos <= query_pos) & ((key_pos < SINK) | (query_pos - key_pos < window))
        term = jnp.where(allowed, 0.0, -1e30)
        for head in range(ratio):
            bias[chunk, pl.ds(head * rows, rows), :] = term

    for copy in small:
        copy.wait()
    for copy in prefix_copies:
        copy.wait_recv()

    def attend(chunk, group):
        lanes = pl.multiple_of(group * (ratio * HEAD), 128)
        mine = jnp.concatenate(
            [
                query[pl.ds(chunk * rows, rows), pl.ds(lanes + head * HEAD, HEAD)]
                for head in range(ratio)
            ],
            axis=0,
        )
        keys_here = rows_kv[:, pl.ds(pl.multiple_of(group * HEAD, 128), HEAD)]
        values = rows_kv[:, pl.ds(pl.multiple_of(kv_cols + group * HEAD, 128), HEAD)]
        scores = lax.dot_general(
            mine, keys_here, (((1,), (1,)), ((), ())), preferred_element_type=jnp.float32
        )
        scores = scores * HEAD ** (-0.5) + bias[chunk]
        expo = jnp.exp(scores - jnp.max(scores, axis=-1, keepdims=True))
        denom = jnp.sum(expo, axis=-1, keepdims=True)
        result = jnp.dot(expo.astype(jnp.bfloat16), values, preferred_element_type=jnp.float32)
        result = (result * (1.0 / denom)).astype(jnp.bfloat16)
        for head in range(ratio):
            attended[chunk, row_slice(r, rows), pl.ds(lanes + head * HEAD, HEAD)] = result[
                head * rows : (head + 1) * rows
            ]

    class Gather:
        def __init__(self, region):
            self.region = region
            base = reserve(14)
            X, Y, S = flip(2), flip(4), flip(1)
            plan = [
                (r, 0, X), (r, 1, Y), (r, 1, X), (r, 0, Y),
                (X, 0, Y), (Y, 1, X),
                (r, 0, S), (r, 1, S),
                (X, 0, S), (Y, 1, S), (X, 1, S), (Y, 0, S),
                (flip(6), 0, S), (flip(6), 1, S),
            ]
            self.copies = [
                remote(region(owner, rail), region(owner, rail), base + i, device)
                for i, (owner, rail, device) in enumerate(plan)
            ]

        def go(self, *which):
            for i in which:
                begin(self.copies[i])

        def got(self, *which):
            for i in which:
                self.copies[i].wait_recv()

        def forward(self):
            self.got(0)
            self.go(4, 8)
            self.got(1)
            self.go(5, 9)
            self.got(2)
            self.go(10)
            self.got(3)
            self.go(11)

        def relay(self):
            self.got(4)
            self.go(12)
            self.got(5)
            self.go(13)

        def finish(self):
            self.got(6, 7, 8, 9, 10, 11, 12, 13)

    def attended_region(chunk):
        return lambda owner, rail: attended.at[chunk, row_slice(owner, rows), pl.ds(rail * half, half)]

    def normed_region(chunk):
        band = n_req * rows // 2
        return lambda owner, rail: normed.at[chunk, pl.ds(rail * band, band), col_slice(owner)]

    heads_gather = [Gather(attended_region(chunk)) for chunk in range(CHUNKS)]
    token_gather = [Gather(normed_region(chunk)) for chunk in range(CHUNKS)]

    for chunk in range(CHUNKS):

        @pl.loop(0, KV_HEADS // 2, unroll=4)
        def _(group):
            attend(chunk, group)

        heads_gather[chunk].go(0, 3, 6)

        @pl.loop(KV_HEADS // 2, KV_HEADS, unroll=4)
        def _(group):
            attend(chunk, group)

        heads_gather[chunk].go(1, 2, 7)
        z_step(2, chunk)

    heads_gather[0].forward()
    z_step(3, 0)
    heads_gather[0].relay()
    heads_gather[1].forward()
    z_step(3, 1)
    heads_gather[1].relay()
    for copy in input_copies:
        copy.wait_recv()
    own_x.wait()
    own_w.wait()
    heads_gather[0].finish()
    heads_gather[1].finish()
    z_step(4, 0)
    z_step(4, 1)

    gain_here = gain[:, col_slice(r)]

    def project(chunk):
        total = jnp.dot(attended[chunk], out_w[...], preferred_element_type=jnp.float32)
        total = total + residual[:, pl.ds(chunk * rows, rows), :].astype(jnp.float32).reshape(
            n_req * rows, cols
        )
        normed[chunk, :, col_slice(r)] = (total * gain_here).astype(jnp.bfloat16)
        token_gather[chunk].go(0, 1, 2, 3, 6, 7)

    def norms(chunk):
        inverse = 1.0 / gain[...]

        @pl.loop(0, n_req)
        def _(block):
            where = row_slice(block, rows)
            values = normed[chunk, where, :].astype(jnp.float32) * inverse
            mean = jnp.sum(values * values, axis=-1, keepdims=True) / width
            row_scale[where, :] = lax.rsqrt(mean + 1e-05)

    tile = 256

    def widen(chunk, start, stop):
        @pl.loop(start, stop)
        def _(i):
            lanes = pl.ds(pl.multiple_of(i * tile, 128), tile)
            gate = jnp.dot(normed[chunk], gate_w[:, lanes], preferred_element_type=jnp.float32)
            upper = jnp.dot(normed[chunk], up_w[:, lanes], preferred_element_type=jnp.float32)
            scale = row_scale[...]
            gate = gate * scale
            hidden[:, lanes] = (gate / (1.0 + jnp.exp(-gate)) * (upper * scale)).astype(jnp.bfloat16)

    span = width // PIECES

    def narrow(chunk, piece):
        @pl.loop(0, span // tile)
        def _(i):
            lanes = pl.ds(pl.multiple_of(piece * span + i * tile, 128), tile)
            part = jnp.dot(hidden[...], down_w[:, lanes], preferred_element_type=jnp.float32)
            parts[chunk, :, :, :, :, lanes] = part.astype(jnp.bfloat16).reshape(2, 2, 2, rows, tile)

    def rail_cols(piece):
        return pl.ds(piece * span, span)

    def scatter_copies(chunk, rail):
        lanes = rail_cols(rail)
        base = reserve(3)
        to_core = remote(
            parts.at[chunk, :, :, 1 - core, :, lanes], sums.at[chunk, :, :, :, lanes], base, flip(1)
        )
        if rail % 2 == 0:
            far = remote(sums.at[chunk, 1 - y, :, :, lanes], first.at[chunk, rail], base + 1, flip(4))
            near = remote(sums.at[chunk, y, 1 - x, :, lanes], second.at[chunk, rail], base + 2, flip(2))
        else:
            far = remote(sums.at[chunk, :, 1 - x, :, lanes], first.at[chunk, rail], base + 1, flip(2))
            near = remote(sums.at[chunk, 1 - y, x, :, lanes], second.at[chunk, rail], base + 2, flip(4))
        return to_core, far, near

    scatter = [[scatter_copies(chunk, rail) for rail in range(PIECES)] for chunk in range(CHUNKS)]

    def f32(value):
        return value.astype(jnp.float32)

    def scatter_core(chunk, rail):
        begin(scatter[chunk][rail][0])

    def scatter_far(chunk, rail):
        lanes = rail_cols(rail)
        scatter[chunk][rail][0].wait_recv()
        for a in (0, 1):
            for b in (0, 1):
                sums[chunk, a, b, :, lanes] = (
                    f32(sums[chunk, a, b, :, lanes]) + f32(parts[chunk, a, b, core, :, lanes])
                ).astype(jnp.bfloat16)
        begin(scatter[chunk][rail][1])

    def scatter_near(chunk, rail):
        lanes = rail_cols(rail)
        scatter[chunk][rail][1].wait_recv()
        for i in (0, 1):
            a, b = (y, i) if rail % 2 == 0 else (i, x)
            sums[chunk, a, b, :, lanes] = (
                f32(sums[chunk, a, b, :, lanes]) + f32(first[chunk, rail, i])
            ).astype(jnp.bfloat16)
        begin(scatter[chunk][rail][2])

    def scatter_end(chunk, rail):
        lanes = rail_cols(rail)
        scatter[chunk][rail][2].wait_recv()
        feed = f32(sums[chunk, y, x, :, lanes]) + f32(second[chunk, rail])
        mixed = f32(normed[chunk, row_slice(r, rows), lanes]) / gain[:, lanes]
        token = lax.broadcasted_iota(jnp.int32, (rows, span), 0) + chunk * rows
        out_ref[pl.ds(chunk * rows, rows), lanes] = jnp.where(
            token < suffix_len[0], mixed + feed, 0.0
        ).astype(jnp.bfloat16)

    tiles = gate_w.shape[1] // tile
    project(0)
    project(1)
    token_gather[0].forward()
    token_gather[0].relay()
    token_gather[0].finish()
    norms(0)
    for copy in weights:
        copy.wait()
    widen(0, 0, tiles // 2)
    token_gather[1].forward()
    widen(0, tiles // 2, tiles)
    token_gather[1].relay()
    for piece in range(PIECES):
        narrow(0, piece)
        scatter_core(0, piece)
        if piece > 0:
            scatter_far(0, piece - 1)
    token_gather[1].finish()
    norms(1)
    scatter_far(0, PIECES - 1)
    widen(1, 0, tiles // 2)
    scatter_near(0, 0)
    scatter_near(0, 1)
    widen(1, tiles // 2, tiles)
    scatter_near(0, 2)
    scatter_near(0, 3)
    for piece in range(PIECES):
        narrow(1, piece)
        scatter_core(1, piece)
        if piece > 0:
            scatter_far(1, piece - 1)
    scatter_near(1, 0)
    scatter_far(1, PIECES - 1)
    for piece in range(PIECES):
        scatter_end(0, piece)
    for piece in range(1, PIECES):
        scatter_near(1, piece)
        scatter_end(1, piece - 1)
    scatter_end(1, PIECES - 1)

    for copy in started:
        copy.wait_send()
    for step in range(1, n_group):
        for part in range(Z_PARTS):
            for direction in (0, 1):

                @pl.when(z_sends(direction, step))
                def _():
                    z_copy(direction, step, part).wait_send()


def fused(n_group, *args):
    (
        layer_input,
        queries,
        suffix_kv,
        past_kv,
        prefix_kv,
        suffix_len,
        past_len,
        out_weight,
        norm_gain,
        gate_weight,
        up_weight,
        down_weight,
    ) = args
    n_req = 8
    tokens, width = queries.shape
    rows = tokens // CHUNKS
    cols = width // n_req
    ff = gate_weight.shape[1]
    keys = n_req * prefix_kv.shape[0] + past_kv.shape[0] + tokens
    bf16, f32 = jnp.bfloat16, jnp.float32
    hbm = pl.BlockSpec(memory_space=pl.ANY)
    smem = pl.BlockSpec(memory_space=pltpu.SMEM)
    vmem = pl.BlockSpec(memory_space=pltpu.VMEM)
    n_copies = 2 * (n_req - 1) + 14 * 2 * CHUNKS + 3 * PIECES * CHUNKS
    span = width // PIECES
    return pl.pallas_call(
        functools.partial(layer_kernel, n_group),
        out_shape=jax.ShapeDtypeStruct((tokens, width), bf16),
        in_specs=[hbm, hbm, hbm, hbm, hbm, smem, smem, hbm, vmem, hbm, hbm, hbm],
        out_specs=vmem,
        scratch_shapes=[
            pltpu.VMEM((tokens, width), bf16),
            pltpu.VMEM((keys, suffix_kv.shape[1]), bf16),
            pltpu.VMEM((CHUNKS, HEADS // KV_HEADS * rows, keys), f32),
            pltpu.VMEM((n_req, tokens, cols), bf16),
            pltpu.VMEM((n_group * out_weight.shape[0], cols), bf16),
            pltpu.VMEM((CHUNKS, n_req * rows, width), bf16),
            pltpu.VMEM((CHUNKS, n_req * rows, width), bf16),
            pltpu.VMEM((width, ff), bf16),
            pltpu.VMEM((width, ff), bf16),
            pltpu.VMEM((ff, width), bf16),
            pltpu.VMEM((n_req * rows, ff), bf16),
            pltpu.VMEM((n_req * rows, 1), f32),
            pltpu.VMEM((CHUNKS, 2, 2, 2, rows, width), bf16),
            pltpu.VMEM((CHUNKS, 2, 2, rows, width), bf16),
            pltpu.VMEM((CHUNKS, PIECES, 2, rows, span), bf16),
            pltpu.VMEM((CHUNKS, PIECES, rows, span), bf16),
            pltpu.SemaphoreType.DMA((9,)),
            pltpu.SemaphoreType.DMA((n_copies,)),
            pltpu.SemaphoreType.DMA((n_copies,)),
            pltpu.SemaphoreType.DMA((2, n_group - 1, Z_PARTS)),
            pltpu.SemaphoreType.DMA((2, n_group - 1, Z_PARTS)),
            pltpu.VMEM((1, width), f32),
        ],
        compiler_params=pltpu.CompilerParams(
            collective_id=0, has_side_effects=True, vmem_limit_bytes=62 * 2**20
        ),
    )(
        layer_input,
        queries,
        suffix_kv,
        past_kv,
        prefix_kv,
        suffix_len,
        past_len,
        out_weight,
        norm_gain,
        gate_weight,
        up_weight,
        down_weight,
    )


def solution(mesh):
    in_specs = (
        P(("group", "req"), None),
        P(("group", "req"), None),
        P(("group", "req"), None),
        P(("group", "req"), None),
        P(("group", "req"), None),
        P(("group", "req")),
        P(("group", "req")),
        P("group", None),
        P(),
        P(None, "req"),
        P(None, "req"),
        P("req", None),
    )
    out_specs = P(("group", "req"), None)
    body = functools.partial(fused, mesh.shape["group"]) if dict(mesh.shape) == {"group": 4, "req": 8} else shards
    return jax.shard_map(body, mesh=mesh, in_specs=in_specs, out_specs=out_specs, check_vma=False)
```

```python
import functools

import jax
import jax.numpy as jnp
from jax import lax
from jax.experimental import pallas as pl
from jax.experimental.pallas import tpu as pltpu
from jax.sharding import PartitionSpec as P

HEADS = 24
KV_HEADS = 8
HEAD = 128
SINK = 4
MESH = pl.DeviceIdType.MESH
CHUNKS = 2
Z_PARTS = 2
PIECES = 4


def absorb(state, query_heads, key_rows, key_pos, key_valid, query_pos, window):
    maxima, totals, sums = state
    count = key_rows.shape[0]
    key_heads = key_rows[:, : KV_HEADS * HEAD].reshape(count, KV_HEADS, HEAD)
    value_heads = key_rows[:, KV_HEADS * HEAD :].reshape(count, KV_HEADS, HEAD)
    scores = jnp.einsum(
        "skgh,nkh->kgsn", query_heads, key_heads, preferred_element_type=jnp.float32
    ) * HEAD ** (-0.5)
    near = query_pos[:, None] - key_pos[None, :] < window
    allowed = (
        key_valid[None, :]
        & (key_pos[None, :] <= query_pos[:, None])
        & ((key_pos[None, :] < SINK) | near)
    )
    scores = jnp.where(allowed, scores, -1e30)
    new_max = jnp.maximum(maxima, jnp.max(scores, axis=-1))
    expo = jnp.where(allowed, jnp.exp(scores - new_max[..., None]), 0.0)
    factor = jnp.exp(maxima - new_max)
    totals = totals * factor + jnp.sum(expo, axis=-1)
    sums = sums * factor[..., None] + jnp.einsum(
        "kgsn,nkh->kgsh", expo.astype(jnp.bfloat16), value_heads, preferred_element_type=jnp.float32
    )
    return (new_max, totals, sums)


def shards(
    layer_input,
    queries,
    suffix_kv,
    past_kv,
    prefix_kv,
    suffix_len,
    past_len,
    out_weight,
    norm_gain,
    gate_weight,
    up_weight,
    down_weight,
):
    rows_here = queries.shape[0]
    past_slots = past_kv.shape[0]
    prefix_total = prefix_kv.shape[0] * lax.axis_size("req")
    window = prefix_total + past_slots // 2
    past_count = past_len[0]
    offsets = jnp.arange(rows_here, dtype=jnp.int32)
    query_pos = prefix_total + past_count + offsets
    ratio = HEADS // KV_HEADS
    query_heads = queries.reshape(rows_here, KV_HEADS, ratio, HEAD)
    state = (
        jnp.full((KV_HEADS, ratio, rows_here), -1e30, jnp.float32),
        jnp.zeros((KV_HEADS, ratio, rows_here), jnp.float32),
        jnp.zeros((KV_HEADS, ratio, rows_here, HEAD), jnp.float32),
    )
    local_rows = jnp.concatenate([past_kv, suffix_kv], axis=0)
    local_pos = jnp.concatenate([prefix_total + jnp.arange(past_slots, dtype=jnp.int32), query_pos])
    local_valid = jnp.concatenate(
        [jnp.arange(past_slots, dtype=jnp.int32) < past_count, jnp.ones((rows_here,), bool)]
    )
    state = absorb(state, query_heads, local_rows, local_pos, local_valid, query_pos, window)
    piece = lax.all_gather(prefix_kv, "req", axis=0, tiled=True)
    count = piece.shape[0]
    positions = jnp.arange(count, dtype=jnp.int32)
    maxima, totals, sums = absorb(
        state, query_heads, piece, positions, jnp.ones((count,), bool), query_pos, window
    )
    attended = (
        (sums / totals[..., None])
        .transpose(2, 0, 1, 3)
        .reshape(rows_here, HEADS * HEAD)
        .astype(jnp.bfloat16)
    )
    blocks = lax.axis_size("group")
    split_rows = attended.reshape(rows_here, blocks, attended.shape[1] // blocks)
    received = lax.all_to_all(split_rows, "group", split_axis=1, concat_axis=0, tiled=True)
    received = received.reshape(blocks * rows_here, attended.shape[1] // blocks)
    picked = received
    projected = lax.psum_scatter(
        jnp.dot(picked, out_weight, preferred_element_type=jnp.float32).astype(jnp.bfloat16),
        "group",
        scatter_dimension=0,
        tiled=True,
    ).astype(jnp.float32)
    mixed = layer_input.astype(jnp.float32) + projected
    scale = lax.rsqrt(jnp.mean(mixed * mixed, axis=-1, keepdims=True) + 1e-05)
    normed = (mixed * scale * norm_gain.astype(jnp.float32)).astype(jnp.bfloat16)
    gathered = lax.all_gather(normed, "req", axis=0, tiled=True)
    picked = gathered
    gate = jnp.dot(picked, gate_weight, preferred_element_type=jnp.float32)
    upper = jnp.dot(picked, up_weight, preferred_element_type=jnp.float32)
    hidden = (jax.nn.silu(gate) * upper).astype(jnp.bfloat16)
    feed = lax.psum_scatter(
        jnp.dot(hidden, down_weight, preferred_element_type=jnp.float32).astype(jnp.bfloat16),
        "req",
        scatter_dimension=0,
        tiled=True,
    ).astype(jnp.float32)
    live = offsets < suffix_len[0]
    return jnp.where(live[:, None], mixed + feed, 0.0).astype(jnp.bfloat16)


def layer_kernel(
    n_group,
    input_hbm,
    query_hbm,
    suffix_hbm,
    past_hbm,
    prefix_hbm,
    suffix_len,
    past_len,
    outw_hbm,
    gain_ref,
    gate_hbm,
    up_hbm,
    down_hbm,
    out_ref,
    query,
    rows_kv,
    bias,
    residual,
    out_w,
    attended,
    normed,
    gate_w,
    up_w,
    down_w,
    hidden,
    row_scale,
    parts,
    sums,
    first,
    second,
    local_sem,
    send_sem,
    recv_sem,
    z_send,
    z_recv,
    gain,
    gate_sum,
    up_sum,
):
    n_req = 8
    z = lax.axis_index("group")
    r = lax.axis_index("req")
    core, x, y = r % 2, (r // 2) % 2, r // 4

    def flip(mask):
        c2 = 1 - core if mask & 1 else core
        x2 = 1 - x if mask & 2 else x
        y2 = 1 - y if mask & 4 else y
        return y2 * 4 + x2 * 2 + c2

    tokens, width = query.shape
    rows = tokens // CHUNKS
    past_slots = past_hbm.shape[0]
    own_prefix = prefix_hbm.shape[0]
    prefix = own_prefix * n_req
    window = prefix + past_slots // 2
    depth = outw_hbm.shape[0]
    cols = width // n_req
    half = width // 2
    kv_cols = KV_HEADS * HEAD
    keys = prefix + past_slots + tokens

    def col_slice(owner):
        return pl.ds(pl.multiple_of(owner * cols, 128), cols)

    def row_slice(owner, count):
        return pl.ds(pl.multiple_of(owner * count, 16), count)

    used = [0]
    started = []

    def reserve(count):
        base = used[0]
        used[0] += count
        return base

    def remote(src, dst, index, device):
        return pltpu.make_async_remote_copy(
            src_ref=src,
            dst_ref=dst,
            send_sem=send_sem.at[index],
            recv_sem=recv_sem.at[index],
            device_id={"req": device},
            device_id_type=MESH,
        )

    def begin(copy):
        copy.start()
        started.append(copy)

    def local(src, dst, index):
        copy = pltpu.make_async_copy(src, dst, local_sem.at[index])
        copy.start()
        return copy

    small = [
        local(query_hbm, query, 0),
        local(past_hbm, rows_kv.at[pl.ds(prefix, past_slots)], 1),
        local(suffix_hbm, rows_kv.at[pl.ds(prefix + past_slots, tokens)], 2),
        local(prefix_hbm, rows_kv.at[row_slice(r, own_prefix)], 3),
    ]
    own_w = local(outw_hbm.at[:, col_slice(r)], out_w.at[row_slice(z, depth)], 4)
    own_x = local(input_hbm.at[:, col_slice(r)], residual.at[r], 5)

    barrier = pltpu.get_barrier_semaphore()
    for mask in range(1, n_req):
        pl.semaphore_signal(barrier, inc=1, device_id={"req": flip(mask)}, device_id_type=MESH)
    has_left, has_right = z > 0, z < n_group - 1

    @pl.when(has_left)
    def _():
        pl.semaphore_signal(barrier, inc=1, device_id={"group": z - 1}, device_id_type=MESH)

    @pl.when(has_right)
    def _():
        pl.semaphore_signal(barrier, inc=1, device_id={"group": z + 1}, device_id_type=MESH)

    peers = n_req - 1 + jnp.where(has_left, 1, 0) + jnp.where(has_right, 1, 0)
    pl.semaphore_wait(barrier, peers)

    prefix_copies = []
    base = reserve(n_req - 1)
    for mask in range(1, n_req):
        copy = remote(prefix_hbm, rows_kv.at[row_slice(r, own_prefix)], base + mask - 1, flip(mask))
        begin(copy)
        prefix_copies.append(copy)

    def z_part(block, part):
        return pl.ds(pl.multiple_of(block * depth + part * (depth // Z_PARTS), 16), depth // Z_PARTS)

    def z_copy(direction, step, part):
        block = z - (step - 1) if direction == 0 else z + (step - 1)
        where = out_w.at[z_part(block, part)]
        src = outw_hbm.at[z_part(0, part), col_slice(r)] if step == 1 else where
        return pltpu.make_async_remote_copy(
            src_ref=src,
            dst_ref=where,
            send_sem=z_send.at[direction, step - 1, part],
            recv_sem=z_recv.at[direction, step - 1, part],
            device_id={"group": z + 1 if direction == 0 else z - 1},
            device_id_type=MESH,
        )

    def z_sends(direction, step):
        if direction == 0:
            return (z - (step - 1) >= 0) & has_right
        return (z + (step - 1) <= n_group - 1) & has_left

    def z_gets(direction, step):
        return z - step >= 0 if direction == 0 else z + step <= n_group - 1

    def z_arrived(direction, step, part):
        block = z - step if direction == 0 else z + step
        where = out_w.at[z_part(block, part)]
        pltpu.make_async_remote_copy(
            src_ref=where,
            dst_ref=where,
            send_sem=z_send.at[direction, step - 1, part],
            recv_sem=z_recv.at[direction, step - 1, part],
            device_id={"req": flip(1)},
            device_id_type=MESH,
        ).wait_recv()

    def z_step(step, part):
        for direction in (0, 1):
            if step > 1:

                @pl.when(z_gets(direction, step - 1))
                def _():
                    z_arrived(direction, step - 1, part)

            if step < n_group:

                @pl.when(z_sends(direction, step))
                def _():
                    z_copy(direction, step, part).start()

    z_step(1, 0)
    z_step(1, 1)

    weights = [
        local(gate_hbm, gate_w, 6),
        local(up_hbm, up_w, 7),
        local(down_hbm, down_w, 8),
    ]

    gain[...] = gain_ref[...].astype(jnp.float32).reshape(gain.shape)

    ratio = HEADS // KV_HEADS
    past_count = past_len[0]
    for chunk in range(CHUNKS):
        key = lax.broadcasted_iota(jnp.int32, (rows, keys), 1)
        token = lax.broadcasted_iota(jnp.int32, (rows, keys), 0) + chunk * rows
        query_pos = prefix + past_count + token
        key_pos = jnp.where(key < prefix + past_slots, key, key - past_slots + past_count)
        valid = (key < prefix + past_count) | (key >= prefix + past_slots)
        allowed = valid & (key_pos <= query_pos) & ((key_pos < SINK) | (query_pos - key_pos < window))
        term = jnp.where(allowed, 0.0, -1e30)
        for head in range(ratio):
            bias[chunk, pl.ds(head * rows, rows), :] = term

    for copy in small:
        copy.wait()
    for copy in prefix_copies:
        copy.wait_recv()

    input_copies = []
    base = reserve(n_req - 1)
    for mask in range(1, n_req):
        other = flip(mask)
        copy = remote(input_hbm.at[:, col_slice(other)], residual.at[r], base + mask - 1, other)
        begin(copy)
        input_copies.append(copy)

    def attend(chunk, group):
        lanes = pl.multiple_of(group * (ratio * HEAD), 128)
        mine = jnp.concatenate(
            [
                query[pl.ds(chunk * rows, rows), pl.ds(lanes + head * HEAD, HEAD)]
                for head in range(ratio)
            ],
            axis=0,
        )
        keys_here = rows_kv[:, pl.ds(pl.multiple_of(group * HEAD, 128), HEAD)]
        values = rows_kv[:, pl.ds(pl.multiple_of(kv_cols + group * HEAD, 128), HEAD)]
        scores = lax.dot_general(
            mine, keys_here, (((1,), (1,)), ((), ())), preferred_element_type=jnp.float32
        )
        scores = scores * HEAD ** (-0.5) + bias[chunk]
        expo = jnp.exp(scores - jnp.max(scores, axis=-1, keepdims=True))
        denom = jnp.sum(expo, axis=-1, keepdims=True)
        result = jnp.dot(expo.astype(jnp.bfloat16), values, preferred_element_type=jnp.float32)
        result = (result * (1.0 / denom)).astype(jnp.bfloat16)
        for head in range(ratio):
            attended[chunk, row_slice(r, rows), pl.ds(lanes + head * HEAD, HEAD)] = result[
                head * rows : (head + 1) * rows
            ]

    class Gather:
        def __init__(self, region):
            self.region = region
            base = reserve(14)
            X, Y, S = flip(2), flip(4), flip(1)
            plan = [
                (r, 0, X), (r, 1, Y), (r, 1, X), (r, 0, Y),
                (X, 0, Y), (Y, 1, X),
                (r, 0, S), (r, 1, S),
                (X, 0, S), (Y, 1, S), (X, 1, S), (Y, 0, S),
                (flip(6), 0, S), (flip(6), 1, S),
            ]
            self.copies = [
                remote(region(owner, rail), region(owner, rail), base + i, device)
                for i, (owner, rail, device) in enumerate(plan)
            ]

        def go(self, *which):
            for i in which:
                begin(self.copies[i])

        def got(self, *which):
            for i in which:
                self.copies[i].wait_recv()

        def forward(self):
            self.got(0)
            self.go(4, 8)
            self.got(1)
            self.go(5, 9)
            self.got(2)
            self.go(10)
            self.got(3)
            self.go(11)

        def relay(self):
            self.got(4)
            self.go(12)
            self.got(5)
            self.go(13)

        def finish(self):
            self.got(6, 7, 8, 9, 10, 11, 12, 13)

    def attended_region(chunk):
        return lambda owner, rail: attended.at[chunk, row_slice(owner, rows), pl.ds(rail * half, half)]

    def normed_region(chunk):
        band = n_req * rows // 2
        return lambda owner, rail: normed.at[chunk, pl.ds(rail * band, band), col_slice(owner)]

    heads_gather = [Gather(attended_region(chunk)) for chunk in range(CHUNKS)]
    token_gather = [Gather(normed_region(chunk)) for chunk in range(CHUNKS)]

    for chunk in range(CHUNKS):

        @pl.loop(0, KV_HEADS // 2, unroll=4)
        def _(group):
            attend(chunk, group)

        heads_gather[chunk].go(0, 3, 6)

        @pl.loop(KV_HEADS // 2, KV_HEADS, unroll=4)
        def _(group):
            attend(chunk, group)

        heads_gather[chunk].go(1, 2, 7)
        z_step(2, chunk)

    heads_gather[0].forward()
    z_step(3, 0)
    heads_gather[0].relay()
    heads_gather[1].forward()
    z_step(3, 1)
    heads_gather[1].relay()
    for copy in input_copies:
        copy.wait_recv()
    own_x.wait()
    own_w.wait()
    heads_gather[0].finish()
    heads_gather[1].finish()
    z_step(4, 0)
    z_step(4, 1)

    gain_here = gain[:, col_slice(r)]

    def project(chunk):
        total = jnp.dot(attended[chunk], out_w[...], preferred_element_type=jnp.float32)
        total = total + residual[:, pl.ds(chunk * rows, rows), :].astype(jnp.float32).reshape(
            n_req * rows, cols
        )
        normed[chunk, :, col_slice(r)] = (total * gain_here).astype(jnp.bfloat16)

    def norms(chunk):
        inverse = 1.0 / gain[...]

        @pl.loop(0, n_req)
        def _(block):
            where = row_slice(block, rows)
            values = normed[chunk, where, :].astype(jnp.float32) * inverse
            mean = jnp.sum(values * values, axis=-1, keepdims=True) / width
            row_scale[where, :] = lax.rsqrt(mean + 1e-05)

    tile = 256

    def activate(gate, upper, lanes):
        scale = row_scale[...]
        gate = gate * scale
        hidden[:, lanes] = (gate / (1.0 + jnp.exp(-gate)) * (upper * scale)).astype(jnp.bfloat16)

    def widen_part(chunk, owner, is_first, is_last):
        depth_here = pl.ds(pl.multiple_of(owner // 2 * (2 * cols), 128), 2 * cols)

        @pl.loop(0, gate_w.shape[1] // tile, unroll=2)
        def _(i):
            lanes = pl.ds(pl.multiple_of(i * tile, 128), tile)
            left = normed[chunk, :, depth_here]
            gate = jnp.dot(left, gate_w[depth_here, lanes], preferred_element_type=jnp.float32)
            upper = jnp.dot(left, up_w[depth_here, lanes], preferred_element_type=jnp.float32)
            if not is_first:
                gate = gate_sum[:, lanes] + gate
                upper = up_sum[:, lanes] + upper
            if is_last:
                activate(gate, upper, lanes)
            else:
                gate_sum[:, lanes] = gate
                up_sum[:, lanes] = upper

    def widen(chunk, start, stop):
        @pl.loop(start, stop, unroll=stop - start)
        def _(i):
            lanes = pl.ds(pl.multiple_of(i * tile, 128), tile)
            gate = jnp.dot(normed[chunk], gate_w[:, lanes], preferred_element_type=jnp.float32)
            upper = jnp.dot(normed[chunk], up_w[:, lanes], preferred_element_type=jnp.float32)
            activate(gate, upper, lanes)

    span = width // PIECES

    def narrow(chunk, piece):
        @pl.loop(0, span // tile, unroll=span // tile)
        def _(i):
            lanes = pl.ds(pl.multiple_of(piece * span + i * tile, 128), tile)
            part = jnp.dot(hidden[...], down_w[:, lanes], preferred_element_type=jnp.float32)
            parts[chunk, :, :, :, :, lanes] = part.astype(jnp.bfloat16).reshape(2, 2, 2, rows, tile)

    def rail_cols(piece):
        return pl.ds(piece * span, span)

    def scatter_copies(chunk, rail):
        lanes = rail_cols(rail)
        base = reserve(3)
        to_core = remote(
            parts.at[chunk, :, :, 1 - core, :, lanes], sums.at[chunk, :, :, :, lanes], base, flip(1)
        )
        if rail % 2 == 0:
            far = remote(sums.at[chunk, 1 - y, :, :, lanes], first.at[chunk, rail], base + 1, flip(4))
            near = remote(sums.at[chunk, y, 1 - x, :, lanes], second.at[chunk, rail], base + 2, flip(2))
        else:
            far = remote(sums.at[chunk, :, 1 - x, :, lanes], first.at[chunk, rail], base + 1, flip(2))
            near = remote(sums.at[chunk, 1 - y, x, :, lanes], second.at[chunk, rail], base + 2, flip(4))
        return to_core, far, near

    scatter = [[scatter_copies(chunk, rail) for rail in range(PIECES)] for chunk in range(CHUNKS)]

    def f32(value):
        return value.astype(jnp.float32)

    def scatter_core(chunk, rail):
        begin(scatter[chunk][rail][0])

    def scatter_far(chunk, rail):
        lanes = rail_cols(rail)
        scatter[chunk][rail][0].wait_recv()
        for a in (0, 1):
            for b in (0, 1):
                sums[chunk, a, b, :, lanes] = (
                    f32(sums[chunk, a, b, :, lanes]) + f32(parts[chunk, a, b, core, :, lanes])
                ).astype(jnp.bfloat16)
        begin(scatter[chunk][rail][1])

    def scatter_near(chunk, rail):
        lanes = rail_cols(rail)
        scatter[chunk][rail][1].wait_recv()
        for i in (0, 1):
            a, b = (y, i) if rail % 2 == 0 else (i, x)
            sums[chunk, a, b, :, lanes] = (
                f32(sums[chunk, a, b, :, lanes]) + f32(first[chunk, rail, i])
            ).astype(jnp.bfloat16)
        begin(scatter[chunk][rail][2])

    def scatter_end(chunk, rail):
        lanes = rail_cols(rail)
        scatter[chunk][rail][2].wait_recv()
        feed = f32(sums[chunk, y, x, :, lanes]) + f32(second[chunk, rail])
        mixed = f32(normed[chunk, row_slice(r, rows), lanes]) / gain[:, lanes]
        token = lax.broadcasted_iota(jnp.int32, (rows, span), 0) + chunk * rows
        out_ref[pl.ds(chunk * rows, rows), lanes] = jnp.where(
            token < suffix_len[0], mixed + feed, 0.0
        ).astype(jnp.bfloat16)

    tiles = gate_w.shape[1] // tile
    order = (0, 1, 2, 3, 6, 7)
    ahead = token_gather[0]
    project(0)
    ahead.go(*order)
    project(1)
    for copy in weights:
        copy.wait()
    ahead.got(6, 7)
    widen_part(0, r, True, False)
    ahead.forward()
    token_gather[1].go(*order)
    ahead.got(8, 10)
    widen_part(0, flip(2), False, False)
    ahead.relay()
    ahead.got(9, 11)
    widen_part(0, flip(4), False, False)
    ahead.got(12, 13)
    norms(0)
    widen_part(0, flip(6), False, True)
    token_gather[1].forward()
    for piece in range(PIECES):
        if piece == 2:
            token_gather[1].relay()
        narrow(0, piece)
        scatter_core(0, piece)
        if piece > 0:
            scatter_far(0, piece - 1)
    token_gather[1].finish()
    norms(1)
    scatter_far(0, PIECES - 1)
    widen(1, 0, tiles // 2)
    scatter_near(0, 0)
    scatter_near(0, 1)
    widen(1, tiles // 2, tiles)
    scatter_near(0, 2)
    scatter_near(0, 3)
    for piece in range(PIECES):
        narrow(1, piece)
        scatter_core(1, piece)
        if piece > 0:
            scatter_far(1, piece - 1)
    scatter_near(1, 0)
    scatter_far(1, PIECES - 1)
    for piece in range(PIECES):
        scatter_end(0, piece)
    for piece in range(1, PIECES):
        scatter_near(1, piece)
        scatter_end(1, piece - 1)
    scatter_end(1, PIECES - 1)

    for copy in started:
        copy.wait_send()
    for step in range(1, n_group):
        for part in range(Z_PARTS):
            for direction in (0, 1):

                @pl.when(z_sends(direction, step))
                def _():
                    z_copy(direction, step, part).wait_send()


def fused(n_group, *args):
    (
        layer_input,
        queries,
        suffix_kv,
        past_kv,
        prefix_kv,
        suffix_len,
        past_len,
        out_weight,
        norm_gain,
        gate_weight,
        up_weight,
        down_weight,
    ) = args
    n_req = 8
    tokens, width = queries.shape
    rows = tokens // CHUNKS
    cols = width // n_req
    ff = gate_weight.shape[1]
    keys = n_req * prefix_kv.shape[0] + past_kv.shape[0] + tokens
    bf16, f32 = jnp.bfloat16, jnp.float32
    hbm = pl.BlockSpec(memory_space=pl.ANY)
    smem = pl.BlockSpec(memory_space=pltpu.SMEM)
    vmem = pl.BlockSpec(memory_space=pltpu.VMEM)
    n_copies = 2 * (n_req - 1) + 14 * 2 * CHUNKS + 3 * PIECES * CHUNKS
    span = width // PIECES
    return pl.pallas_call(
        functools.partial(layer_kernel, n_group),
        out_shape=jax.ShapeDtypeStruct((tokens, width), bf16),
        in_specs=[hbm, hbm, hbm, hbm, hbm, smem, smem, hbm, vmem, hbm, hbm, hbm],
        out_specs=vmem,
        scratch_shapes=[
            pltpu.VMEM((tokens, width), bf16),
            pltpu.VMEM((keys, suffix_kv.shape[1]), bf16),
            pltpu.VMEM((CHUNKS, HEADS // KV_HEADS * rows, keys), f32),
            pltpu.VMEM((n_req, tokens, cols), bf16),
            pltpu.VMEM((n_group * out_weight.shape[0], cols), bf16),
            pltpu.VMEM((CHUNKS, n_req * rows, width), bf16),
            pltpu.VMEM((CHUNKS, n_req * rows, width), bf16),
            pltpu.VMEM((width, ff), bf16),
            pltpu.VMEM((width, ff), bf16),
            pltpu.VMEM((ff, width), bf16),
            pltpu.VMEM((n_req * rows, ff), bf16),
            pltpu.VMEM((n_req * rows, 1), f32),
            pltpu.VMEM((CHUNKS, 2, 2, 2, rows, width), bf16),
            pltpu.VMEM((CHUNKS, 2, 2, rows, width), bf16),
            pltpu.VMEM((CHUNKS, PIECES, 2, rows, span), bf16),
            pltpu.VMEM((CHUNKS, PIECES, rows, span), bf16),
            pltpu.SemaphoreType.DMA((9,)),
            pltpu.SemaphoreType.DMA((n_copies,)),
            pltpu.SemaphoreType.DMA((n_copies,)),
            pltpu.SemaphoreType.DMA((2, n_group - 1, Z_PARTS)),
            pltpu.SemaphoreType.DMA((2, n_group - 1, Z_PARTS)),
            pltpu.VMEM((1, width), f32),
            pltpu.VMEM((n_req * rows, ff), f32),
            pltpu.VMEM((n_req * rows, ff), f32),
        ],
        compiler_params=pltpu.CompilerParams(
            collective_id=0, has_side_effects=True, vmem_limit_bytes=62 * 2**20
        ),
    )(
        layer_input,
        queries,
        suffix_kv,
        past_kv,
        prefix_kv,
        suffix_len,
        past_len,
        out_weight,
        norm_gain,
        gate_weight,
        up_weight,
        down_weight,
    )


def solution(mesh):
    in_specs = (
        P(("group", "req"), None),
        P(("group", "req"), None),
        P(("group", "req"), None),
        P(("group", "req"), None),
        P(("group", "req"), None),
        P(("group", "req")),
        P(("group", "req")),
        P("group", None),
        P(),
        P(None, "req"),
        P(None, "req"),
        P("req", None),
    )
    out_specs = P(("group", "req"), None)
    body = functools.partial(fused, mesh.shape["group"]) if dict(mesh.shape) == {"group": 4, "req": 8} else shards
    return jax.shard_map(body, mesh=mesh, in_specs=in_specs, out_specs=out_specs, check_vma=False)
```

```python
import functools

import jax
import jax.numpy as jnp
from jax import lax
from jax.experimental import pallas as pl
from jax.experimental.pallas import tpu as pltpu
from jax.sharding import PartitionSpec as P

HEADS = 24
KV_HEADS = 8
HEAD = 128
SINK = 4
MESH = pl.DeviceIdType.MESH
CHUNKS = 2
Z_PARTS = 2
PIECES = 6


def absorb(state, query_heads, key_rows, key_pos, key_valid, query_pos, window):
    maxima, totals, sums = state
    count = key_rows.shape[0]
    key_heads = key_rows[:, : KV_HEADS * HEAD].reshape(count, KV_HEADS, HEAD)
    value_heads = key_rows[:, KV_HEADS * HEAD :].reshape(count, KV_HEADS, HEAD)
    scores = jnp.einsum(
        "skgh,nkh->kgsn", query_heads, key_heads, preferred_element_type=jnp.float32
    ) * HEAD ** (-0.5)
    near = query_pos[:, None] - key_pos[None, :] < window
    allowed = (
        key_valid[None, :]
        & (key_pos[None, :] <= query_pos[:, None])
        & ((key_pos[None, :] < SINK) | near)
    )
    scores = jnp.where(allowed, scores, -1e30)
    new_max = jnp.maximum(maxima, jnp.max(scores, axis=-1))
    expo = jnp.where(allowed, jnp.exp(scores - new_max[..., None]), 0.0)
    factor = jnp.exp(maxima - new_max)
    totals = totals * factor + jnp.sum(expo, axis=-1)
    sums = sums * factor[..., None] + jnp.einsum(
        "kgsn,nkh->kgsh", expo.astype(jnp.bfloat16), value_heads, preferred_element_type=jnp.float32
    )
    return (new_max, totals, sums)


def shards(
    layer_input,
    queries,
    suffix_kv,
    past_kv,
    prefix_kv,
    suffix_len,
    past_len,
    out_weight,
    norm_gain,
    gate_weight,
    up_weight,
    down_weight,
):
    rows_here = queries.shape[0]
    past_slots = past_kv.shape[0]
    prefix_total = prefix_kv.shape[0] * lax.axis_size("req")
    window = prefix_total + past_slots // 2
    past_count = past_len[0]
    offsets = jnp.arange(rows_here, dtype=jnp.int32)
    query_pos = prefix_total + past_count + offsets
    ratio = HEADS // KV_HEADS
    query_heads = queries.reshape(rows_here, KV_HEADS, ratio, HEAD)
    state = (
        jnp.full((KV_HEADS, ratio, rows_here), -1e30, jnp.float32),
        jnp.zeros((KV_HEADS, ratio, rows_here), jnp.float32),
        jnp.zeros((KV_HEADS, ratio, rows_here, HEAD), jnp.float32),
    )
    local_rows = jnp.concatenate([past_kv, suffix_kv], axis=0)
    local_pos = jnp.concatenate([prefix_total + jnp.arange(past_slots, dtype=jnp.int32), query_pos])
    local_valid = jnp.concatenate(
        [jnp.arange(past_slots, dtype=jnp.int32) < past_count, jnp.ones((rows_here,), bool)]
    )
    state = absorb(state, query_heads, local_rows, local_pos, local_valid, query_pos, window)
    piece = lax.all_gather(prefix_kv, "req", axis=0, tiled=True)
    count = piece.shape[0]
    positions = jnp.arange(count, dtype=jnp.int32)
    maxima, totals, sums = absorb(
        state, query_heads, piece, positions, jnp.ones((count,), bool), query_pos, window
    )
    attended = (
        (sums / totals[..., None])
        .transpose(2, 0, 1, 3)
        .reshape(rows_here, HEADS * HEAD)
        .astype(jnp.bfloat16)
    )
    blocks = lax.axis_size("group")
    split_rows = attended.reshape(rows_here, blocks, attended.shape[1] // blocks)
    received = lax.all_to_all(split_rows, "group", split_axis=1, concat_axis=0, tiled=True)
    received = received.reshape(blocks * rows_here, attended.shape[1] // blocks)
    picked = received
    projected = lax.psum_scatter(
        jnp.dot(picked, out_weight, preferred_element_type=jnp.float32).astype(jnp.bfloat16),
        "group",
        scatter_dimension=0,
        tiled=True,
    ).astype(jnp.float32)
    mixed = layer_input.astype(jnp.float32) + projected
    scale = lax.rsqrt(jnp.mean(mixed * mixed, axis=-1, keepdims=True) + 1e-05)
    normed = (mixed * scale * norm_gain.astype(jnp.float32)).astype(jnp.bfloat16)
    gathered = lax.all_gather(normed, "req", axis=0, tiled=True)
    picked = gathered
    gate = jnp.dot(picked, gate_weight, preferred_element_type=jnp.float32)
    upper = jnp.dot(picked, up_weight, preferred_element_type=jnp.float32)
    hidden = (jax.nn.silu(gate) * upper).astype(jnp.bfloat16)
    feed = lax.psum_scatter(
        jnp.dot(hidden, down_weight, preferred_element_type=jnp.float32).astype(jnp.bfloat16),
        "req",
        scatter_dimension=0,
        tiled=True,
    ).astype(jnp.float32)
    live = offsets < suffix_len[0]
    return jnp.where(live[:, None], mixed + feed, 0.0).astype(jnp.bfloat16)


def layer_kernel(
    n_group,
    input_hbm,
    query_hbm,
    suffix_hbm,
    past_hbm,
    prefix_hbm,
    suffix_len,
    past_len,
    outw_hbm,
    gain_ref,
    gate_hbm,
    up_hbm,
    down_hbm,
    out_ref,
    query,
    rows_kv,
    bias,
    residual,
    out_w,
    attended,
    normed,
    gate_w,
    up_w,
    down_w,
    hidden,
    row_scale,
    parts,
    sums,
    first,
    second,
    local_sem,
    send_sem,
    recv_sem,
    z_send,
    z_recv,
    gain,
    gate_sum,
    up_sum,
):
    n_req = 8
    z = lax.axis_index("group")
    r = lax.axis_index("req")
    core, x, y = r % 2, (r // 2) % 2, r // 4

    def flip(mask):
        c2 = 1 - core if mask & 1 else core
        x2 = 1 - x if mask & 2 else x
        y2 = 1 - y if mask & 4 else y
        return y2 * 4 + x2 * 2 + c2

    tokens, width = query.shape
    rows = tokens // CHUNKS
    past_slots = past_hbm.shape[0]
    own_prefix = prefix_hbm.shape[0]
    prefix = own_prefix * n_req
    window = prefix + past_slots // 2
    depth = outw_hbm.shape[0]
    cols = width // n_req
    half = width // 2
    kv_cols = KV_HEADS * HEAD
    keys = prefix + past_slots + tokens

    def col_slice(owner):
        return pl.ds(pl.multiple_of(owner * cols, 128), cols)

    def row_slice(owner, count):
        return pl.ds(pl.multiple_of(owner * count, 16), count)

    used = [0]
    started = []

    def reserve(count):
        base = used[0]
        used[0] += count
        return base

    def remote(src, dst, index, device):
        return pltpu.make_async_remote_copy(
            src_ref=src,
            dst_ref=dst,
            send_sem=send_sem.at[index],
            recv_sem=recv_sem.at[index],
            device_id={"req": device},
            device_id_type=MESH,
        )

    def begin(copy):
        copy.start()
        started.append(copy)

    def local(src, dst, index):
        copy = pltpu.make_async_copy(src, dst, local_sem.at[index])
        copy.start()
        return copy

    small = [
        local(query_hbm, query, 0),
        local(past_hbm, rows_kv.at[pl.ds(prefix, past_slots)], 1),
        local(suffix_hbm, rows_kv.at[pl.ds(prefix + past_slots, tokens)], 2),
        local(prefix_hbm, rows_kv.at[row_slice(r, own_prefix)], 3),
    ]
    own_w = local(outw_hbm.at[:, col_slice(r)], out_w.at[row_slice(z, depth)], 4)
    own_x = local(input_hbm.at[:, col_slice(r)], residual.at[r], 5)

    barrier = pltpu.get_barrier_semaphore()
    for mask in range(1, n_req):
        pl.semaphore_signal(barrier, inc=1, device_id={"req": flip(mask)}, device_id_type=MESH)
    has_left, has_right = z > 0, z < n_group - 1

    @pl.when(has_left)
    def _():
        pl.semaphore_signal(barrier, inc=1, device_id={"group": z - 1}, device_id_type=MESH)

    @pl.when(has_right)
    def _():
        pl.semaphore_signal(barrier, inc=1, device_id={"group": z + 1}, device_id_type=MESH)

    peers = n_req - 1 + jnp.where(has_left, 1, 0) + jnp.where(has_right, 1, 0)
    pl.semaphore_wait(barrier, peers)

    prefix_copies = []
    base = reserve(n_req - 1)
    for mask in range(1, n_req):
        copy = remote(prefix_hbm, rows_kv.at[row_slice(r, own_prefix)], base + mask - 1, flip(mask))
        begin(copy)
        prefix_copies.append(copy)

    def z_part(block, part):
        return pl.ds(pl.multiple_of(block * depth + part * (depth // Z_PARTS), 16), depth // Z_PARTS)

    def z_copy(direction, step, part):
        block = z - (step - 1) if direction == 0 else z + (step - 1)
        where = out_w.at[z_part(block, part)]
        src = outw_hbm.at[z_part(0, part), col_slice(r)] if step == 1 else where
        return pltpu.make_async_remote_copy(
            src_ref=src,
            dst_ref=where,
            send_sem=z_send.at[direction, step - 1, part],
            recv_sem=z_recv.at[direction, step - 1, part],
            device_id={"group": z + 1 if direction == 0 else z - 1},
            device_id_type=MESH,
        )

    def z_sends(direction, step):
        if direction == 0:
            return (z - (step - 1) >= 0) & has_right
        return (z + (step - 1) <= n_group - 1) & has_left

    def z_gets(direction, step):
        return z - step >= 0 if direction == 0 else z + step <= n_group - 1

    def z_arrived(direction, step, part):
        block = z - step if direction == 0 else z + step
        where = out_w.at[z_part(block, part)]
        pltpu.make_async_remote_copy(
            src_ref=where,
            dst_ref=where,
            send_sem=z_send.at[direction, step - 1, part],
            recv_sem=z_recv.at[direction, step - 1, part],
            device_id={"req": flip(1)},
            device_id_type=MESH,
        ).wait_recv()

    def z_step(step, part):
        for direction in (0, 1):
            if step > 1:

                @pl.when(z_gets(direction, step - 1))
                def _():
                    z_arrived(direction, step - 1, part)

            if step < n_group:

                @pl.when(z_sends(direction, step))
                def _():
                    z_copy(direction, step, part).start()

    z_step(1, 0)
    z_step(1, 1)

    weights = [
        local(gate_hbm, gate_w, 6),
        local(up_hbm, up_w, 7),
        local(down_hbm, down_w, 8),
    ]

    gain[...] = gain_ref[...].astype(jnp.float32).reshape(gain.shape)

    ratio = HEADS // KV_HEADS
    past_count = past_len[0]
    for chunk in range(CHUNKS):
        key = lax.broadcasted_iota(jnp.int32, (rows, keys), 1)
        token = lax.broadcasted_iota(jnp.int32, (rows, keys), 0) + chunk * rows
        query_pos = prefix + past_count + token
        key_pos = jnp.where(key < prefix + past_slots, key, key - past_slots + past_count)
        valid = (key < prefix + past_count) | (key >= prefix + past_slots)
        allowed = valid & (key_pos <= query_pos) & ((key_pos < SINK) | (query_pos - key_pos < window))
        term = jnp.where(allowed, 0.0, -1e30)
        for head in range(ratio):
            bias[chunk, pl.ds(head * rows, rows), :] = term

    for copy in small:
        copy.wait()
    for copy in prefix_copies:
        copy.wait_recv()

    input_copies = []
    base = reserve(n_req - 1)
    for mask in range(1, n_req):
        other = flip(mask)
        copy = remote(input_hbm.at[:, col_slice(other)], residual.at[r], base + mask - 1, other)
        begin(copy)
        input_copies.append(copy)

    def attend(chunk, group):
        lanes = pl.multiple_of(group * (ratio * HEAD), 128)
        mine = jnp.concatenate(
            [
                query[pl.ds(chunk * rows, rows), pl.ds(lanes + head * HEAD, HEAD)]
                for head in range(ratio)
            ],
            axis=0,
        )
        keys_here = rows_kv[:, pl.ds(pl.multiple_of(group * HEAD, 128), HEAD)]
        values = rows_kv[:, pl.ds(pl.multiple_of(kv_cols + group * HEAD, 128), HEAD)]
        scores = lax.dot_general(
            mine, keys_here, (((1,), (1,)), ((), ())), preferred_element_type=jnp.float32
        )
        scores = scores * HEAD ** (-0.5) + bias[chunk]
        expo = jnp.exp(scores - jnp.max(scores, axis=-1, keepdims=True))
        denom = jnp.sum(expo, axis=-1, keepdims=True)
        result = jnp.dot(expo.astype(jnp.bfloat16), values, preferred_element_type=jnp.float32)
        result = (result * (1.0 / denom)).astype(jnp.bfloat16)
        for head in range(ratio):
            attended[chunk, row_slice(r, rows), pl.ds(lanes + head * HEAD, HEAD)] = result[
                head * rows : (head + 1) * rows
            ]

    class Gather:
        def __init__(self, region):
            self.region = region
            base = reserve(14)
            X, Y, S = flip(2), flip(4), flip(1)
            plan = [
                (r, 0, X), (r, 1, Y), (r, 1, X), (r, 0, Y),
                (X, 0, Y), (Y, 1, X),
                (r, 0, S), (r, 1, S),
                (X, 0, S), (Y, 1, S), (X, 1, S), (Y, 0, S),
                (flip(6), 0, S), (flip(6), 1, S),
            ]
            self.copies = [
                remote(region(owner, rail), region(owner, rail), base + i, device)
                for i, (owner, rail, device) in enumerate(plan)
            ]

        def go(self, *which):
            for i in which:
                begin(self.copies[i])

        def got(self, *which):
            for i in which:
                self.copies[i].wait_recv()

        def forward(self):
            self.got(0)
            self.go(4, 8)
            self.got(1)
            self.go(5, 9)
            self.got(2)
            self.go(10)
            self.got(3)
            self.go(11)

        def relay(self):
            self.got(4)
            self.go(12)
            self.got(5)
            self.go(13)

        def finish(self):
            self.got(6, 7, 8, 9, 10, 11, 12, 13)

    def attended_region(chunk):
        return lambda owner, rail: attended.at[chunk, row_slice(owner, rows), pl.ds(rail * half, half)]

    def normed_region(chunk):
        band = n_req * rows // 2
        return lambda owner, rail: normed.at[chunk, pl.ds(rail * band, band), col_slice(owner)]

    heads_gather = [Gather(attended_region(chunk)) for chunk in range(CHUNKS)]
    token_gather = [Gather(normed_region(chunk)) for chunk in range(CHUNKS)]

    for chunk in range(CHUNKS):

        @pl.loop(0, KV_HEADS // 2, unroll=4)
        def _(group):
            attend(chunk, group)

        heads_gather[chunk].go(0, 3, 6)

        @pl.loop(KV_HEADS // 2, KV_HEADS, unroll=4)
        def _(group):
            attend(chunk, group)

        heads_gather[chunk].go(1, 2, 7)
        z_step(2, chunk)

    heads_gather[0].forward()
    z_step(3, 0)
    heads_gather[0].relay()
    heads_gather[1].forward()
    z_step(3, 1)
    heads_gather[1].relay()
    for copy in input_copies:
        copy.wait_recv()
    own_x.wait()
    own_w.wait()
    heads_gather[0].finish()
    heads_gather[1].finish()

    def project_part(chunk, block):
        lanes = pl.ds(chunk * cols, cols)
        depth_here = pl.ds(pl.multiple_of(block * depth, 128), depth)
        gate_sum[:, lanes] += jnp.dot(
            attended[chunk, :, depth_here], out_w[depth_here, :], preferred_element_type=jnp.float32
        )

    for chunk in range(CHUNKS):
        gate_sum[:, pl.ds(chunk * cols, cols)] = (
            residual[:, pl.ds(chunk * rows, rows), :].astype(jnp.float32).reshape(n_req * rows, cols)
        )
        project_part(chunk, z)

    for step in range(1, n_group):
        if step == n_group - 1:
            z_step(4, 0)
            z_step(4, 1)
        for direction in (0, 1):

            @pl.when(z_gets(direction, step))
            def _():
                for chunk in range(CHUNKS):
                    project_part(chunk, z - step if direction == 0 else z + step)


    gain_here = gain[:, col_slice(r)]

    def project(chunk):
        total = gate_sum[:, pl.ds(chunk * cols, cols)]
        normed[chunk, :, col_slice(r)] = (total * gain_here).astype(jnp.bfloat16)

    def norms(chunk):
        inverse = 1.0 / gain[...]

        @pl.loop(0, n_req)
        def _(block):
            where = row_slice(block, rows)
            values = normed[chunk, where, :].astype(jnp.float32) * inverse
            mean = jnp.sum(values * values, axis=-1, keepdims=True) / width
            row_scale[where, :] = lax.rsqrt(mean + 1e-05)

    tile = 256

    def activate(gate, upper, lanes):
        scale = row_scale[...]
        gate = gate * scale
        hidden[:, lanes] = (gate / (1.0 + jnp.exp(-gate)) * (upper * scale)).astype(jnp.bfloat16)

    def widen_part(chunk, owner, is_first, is_last):
        depth_here = pl.ds(pl.multiple_of(owner // 2 * (2 * cols), 128), 2 * cols)

        @pl.loop(0, gate_w.shape[1] // tile, unroll=2)
        def _(i):
            lanes = pl.ds(pl.multiple_of(i * tile, 128), tile)
            left = normed[chunk, :, depth_here]
            gate = jnp.dot(left, gate_w[depth_here, lanes], preferred_element_type=jnp.float32)
            upper = jnp.dot(left, up_w[depth_here, lanes], preferred_element_type=jnp.float32)
            if not is_first:
                gate = gate_sum[:, lanes] + gate
                upper = up_sum[:, lanes] + upper
            if is_last:
                activate(gate, upper, lanes)
            else:
                gate_sum[:, lanes] = gate
                up_sum[:, lanes] = upper

    def widen(chunk, start, stop):
        @pl.loop(start, stop, unroll=stop - start)
        def _(i):
            lanes = pl.ds(pl.multiple_of(i * tile, 128), tile)
            gate = jnp.dot(normed[chunk], gate_w[:, lanes], preferred_element_type=jnp.float32)
            upper = jnp.dot(normed[chunk], up_w[:, lanes], preferred_element_type=jnp.float32)
            activate(gate, upper, lanes)

    span = width // PIECES

    def narrow(chunk, piece):
        @pl.loop(0, span // tile, unroll=span // tile)
        def _(i):
            lanes = pl.ds(pl.multiple_of(piece * span + i * tile, 128), tile)
            part = jnp.dot(hidden[...], down_w[:, lanes], preferred_element_type=jnp.float32)
            parts[chunk, :, :, :, :, lanes] = part.astype(jnp.bfloat16).reshape(2, 2, 2, rows, tile)

    def rail_cols(piece):
        return pl.ds(piece * span, span)

    def scatter_copies(chunk, rail):
        lanes = rail_cols(rail)
        base = reserve(3)
        to_core = remote(
            parts.at[chunk, :, :, 1 - core, :, lanes], sums.at[chunk, :, :, :, lanes], base, flip(1)
        )
        if rail % 2 == 0:
            far = remote(sums.at[chunk, 1 - y, :, :, lanes], first.at[chunk, rail], base + 1, flip(4))
            near = remote(sums.at[chunk, y, 1 - x, :, lanes], second.at[chunk, rail], base + 2, flip(2))
        else:
            far = remote(sums.at[chunk, :, 1 - x, :, lanes], first.at[chunk, rail], base + 1, flip(2))
            near = remote(sums.at[chunk, 1 - y, x, :, lanes], second.at[chunk, rail], base + 2, flip(4))
        return to_core, far, near

    scatter = [[scatter_copies(chunk, rail) for rail in range(PIECES)] for chunk in range(CHUNKS)]

    def f32(value):
        return value.astype(jnp.float32)

    def scatter_core(chunk, rail):
        begin(scatter[chunk][rail][0])

    def scatter_far(chunk, rail):
        lanes = rail_cols(rail)
        scatter[chunk][rail][0].wait_recv()
        for a in (0, 1):
            for b in (0, 1):
                sums[chunk, a, b, :, lanes] = (
                    f32(sums[chunk, a, b, :, lanes]) + f32(parts[chunk, a, b, core, :, lanes])
                ).astype(jnp.bfloat16)
        begin(scatter[chunk][rail][1])

    def scatter_near(chunk, rail):
        lanes = rail_cols(rail)
        scatter[chunk][rail][1].wait_recv()
        for i in (0, 1):
            a, b = (y, i) if rail % 2 == 0 else (i, x)
            sums[chunk, a, b, :, lanes] = (
                f32(sums[chunk, a, b, :, lanes]) + f32(first[chunk, rail, i])
            ).astype(jnp.bfloat16)
        begin(scatter[chunk][rail][2])

    def scatter_end(chunk, rail):
        lanes = rail_cols(rail)
        scatter[chunk][rail][2].wait_recv()
        feed = f32(sums[chunk, y, x, :, lanes]) + f32(second[chunk, rail])
        mixed = f32(normed[chunk, row_slice(r, rows), lanes]) / gain[:, lanes]
        token = lax.broadcasted_iota(jnp.int32, (rows, span), 0) + chunk * rows
        out_ref[pl.ds(chunk * rows, rows), lanes] = jnp.where(
            token < suffix_len[0], mixed + feed, 0.0
        ).astype(jnp.bfloat16)

    tiles = gate_w.shape[1] // tile
    order = (0, 1, 2, 3, 6, 7)
    ahead = token_gather[0]
    project(0)
    ahead.go(*order)
    project(1)
    for copy in weights:
        copy.wait()
    ahead.got(6, 7)
    widen_part(0, r, True, False)
    ahead.forward()
    token_gather[1].go(*order)
    ahead.got(8, 10)
    widen_part(0, flip(2), False, False)
    ahead.relay()
    ahead.got(9, 11)
    widen_part(0, flip(4), False, False)
    token_gather[1].forward()
    ahead.got(12, 13)
    norms(0)
    widen_part(0, flip(6), False, True)
    for piece in range(PIECES):
        if piece == 2:
            token_gather[1].relay()
        narrow(0, piece)
        scatter_core(0, piece)
        if piece > 0:
            scatter_far(0, piece - 1)
    token_gather[1].finish()
    norms(1)
    scatter_far(0, PIECES - 1)
    widen(1, 0, tiles // 2)
    for piece in range(PIECES // 2):
        scatter_near(0, piece)
    widen(1, tiles // 2, tiles)
    for piece in range(PIECES // 2, PIECES):
        scatter_near(0, piece)
    for piece in range(PIECES):
        narrow(1, piece)
        scatter_core(1, piece)
        if piece > 0:
            scatter_far(1, piece - 1)
    scatter_far(1, PIECES - 1)
    scatter_near(1, 0)
    scatter_near(1, 1)
    for piece in range(PIECES):
        scatter_end(0, piece)
    for piece in range(2, PIECES):
        scatter_near(1, piece)
        scatter_end(1, piece - 2)
    scatter_end(1, PIECES - 2)
    scatter_end(1, PIECES - 1)

    for copy in started:
        copy.wait_send()
    for step in range(1, n_group):
        for part in range(Z_PARTS):
            for direction in (0, 1):

                @pl.when(z_sends(direction, step))
                def _():
                    z_copy(direction, step, part).wait_send()


def fused(n_group, *args):
    (
        layer_input,
        queries,
        suffix_kv,
        past_kv,
        prefix_kv,
        suffix_len,
        past_len,
        out_weight,
        norm_gain,
        gate_weight,
        up_weight,
        down_weight,
    ) = args
    n_req = 8
    tokens, width = queries.shape
    rows = tokens // CHUNKS
    cols = width // n_req
    ff = gate_weight.shape[1]
    keys = n_req * prefix_kv.shape[0] + past_kv.shape[0] + tokens
    bf16, f32 = jnp.bfloat16, jnp.float32
    hbm = pl.BlockSpec(memory_space=pl.ANY)
    smem = pl.BlockSpec(memory_space=pltpu.SMEM)
    vmem = pl.BlockSpec(memory_space=pltpu.VMEM)
    n_copies = 2 * (n_req - 1) + 14 * 2 * CHUNKS + 3 * PIECES * CHUNKS
    span = width // PIECES
    return pl.pallas_call(
        functools.partial(layer_kernel, n_group),
        out_shape=jax.ShapeDtypeStruct((tokens, width), bf16),
        in_specs=[hbm, hbm, hbm, hbm, hbm, smem, smem, hbm, vmem, hbm, hbm, hbm],
        out_specs=vmem,
        scratch_shapes=[
            pltpu.VMEM((tokens, width), bf16),
            pltpu.VMEM((keys, suffix_kv.shape[1]), bf16),
            pltpu.VMEM((CHUNKS, HEADS // KV_HEADS * rows, keys), f32),
            pltpu.VMEM((n_req, tokens, cols), bf16),
            pltpu.VMEM((n_group * out_weight.shape[0], cols), bf16),
            pltpu.VMEM((CHUNKS, n_req * rows, width), bf16),
            pltpu.VMEM((CHUNKS, n_req * rows, width), bf16),
            pltpu.VMEM((width, ff), bf16),
            pltpu.VMEM((width, ff), bf16),
            pltpu.VMEM((ff, width), bf16),
            pltpu.VMEM((n_req * rows, ff), bf16),
            pltpu.VMEM((n_req * rows, 1), f32),
            pltpu.VMEM((CHUNKS, 2, 2, 2, rows, width), bf16),
            pltpu.VMEM((CHUNKS, 2, 2, rows, width), bf16),
            pltpu.VMEM((CHUNKS, PIECES, 2, rows, span), bf16),
            pltpu.VMEM((CHUNKS, PIECES, rows, span), bf16),
            pltpu.SemaphoreType.DMA((9,)),
            pltpu.SemaphoreType.DMA((n_copies,)),
            pltpu.SemaphoreType.DMA((n_copies,)),
            pltpu.SemaphoreType.DMA((2, n_group - 1, Z_PARTS)),
            pltpu.SemaphoreType.DMA((2, n_group - 1, Z_PARTS)),
            pltpu.VMEM((1, width), f32),
            pltpu.VMEM((n_req * rows, ff), f32),
            pltpu.VMEM((n_req * rows, ff), f32),
        ],
        compiler_params=pltpu.CompilerParams(
            collective_id=0, has_side_effects=True, vmem_limit_bytes=62 * 2**20
        ),
    )(
        layer_input,
        queries,
        suffix_kv,
        past_kv,
        prefix_kv,
        suffix_len,
        past_len,
        out_weight,
        norm_gain,
        gate_weight,
        up_weight,
        down_weight,
    )


def solution(mesh):
    in_specs = (
        P(("group", "req"), None),
        P(("group", "req"), None),
        P(("group", "req"), None),
        P(("group", "req"), None),
        P(("group", "req"), None),
        P(("group", "req")),
        P(("group", "req")),
        P("group", None),
        P(),
        P(None, "req"),
        P(None, "req"),
        P("req", None),
    )
    out_specs = P(("group", "req"), None)
    body = functools.partial(fused, mesh.shape["group"]) if dict(mesh.shape) == {"group": 4, "req": 8} else shards
    return jax.shard_map(body, mesh=mesh, in_specs=in_specs, out_specs=out_specs, check_vma=False)
```
